32 devices in a mesh: rows: 8 (over y, x, core), ch: 4 (over z).
Axes of the slice: x: 2, y: 2, z: 4, core: 2. Of those that a mesh axis runs over, the one named last changes fastest.
Arguments:
- field: float32 [2, 128, 32, 1024], P(None, 'ch', 'rows'), may hold values from -6 to 6
- cotangent: float32 [2, 128, 32, 1024], P(None, 'ch', 'rows'), may hold values from -3 to 3
- weight: float32 [32, 128, 128, 128], P('rows', 'ch'), may hold values from -0.75 to 0.75
- bias: float32 [128], replicated, may hold values from -3 to 3
- mode_rows: int32 [32], replicated, may hold values from 0 to 31, as said below
- mode_cols: int32 [64], replicated, may hold values from 0 to 1023, as said below
Outputs:
- grad_field: float32 [2, 128, 32, 1024], P(None, 'ch', 'rows')
- grad_weight: float32 [32, 128, 128, 128], P('rows', 'ch')
The draws below stay inside these ranges and needn't reach their ends.
Inputs may be any that keep to these rules, and one draw needn't show every extreme that they name: `mode_rows`: 32 distinct values; 0 and 31 are among them. `mode_cols`: 64 distinct values; 0 and 1023 are among them.
All inputs are finite; a program needn't handle non-finite values.
Results may differ from the reference program's by a relative error of at most 0.0003.
Values sent between devices are 32-bit elements; how exact they have to be, the bound alone decides.
A program may use at most 64 MiB of HBM per device.

```python
import math
import jax
import jax.numpy as jnp
from jax import lax

SAMPLES = 2
WIDTH = 128
GRID_W = 1024
MODES_H = 32
MODES_W = 64
GRID_H = 32


def pick_modes(key, length, count):
    inner = jax.random.permutation(key, length - 2)[:count - 2].astype(jnp.int32) + 1
    first = jnp.zeros((1,), jnp.int32)
    last = jnp.full((1,), length - 1, jnp.int32)
    return jnp.concatenate([first, inner, last])


def draw_mode_rows(key, part):
    return pick_modes(jax.random.fold_in(key, 11), GRID_H, MODES_H)


def draw_mode_cols(key, part):
    return pick_modes(jax.random.fold_in(key, 23), GRID_W, MODES_W)


def with_spikes(drawn, rng, source, target, parts, factor):
    owner, partner = [(jnp.arange(drawn.shape[dim]) // (drawn.shape[dim] // parts)).reshape([-1 if axis == dim else 1 for axis in range(drawn.ndim)]) for dim in (source, target)]
    chosen = jax.random.permutation(rng, parts)[partner]
    strong = (owner == chosen) | (owner == (partner + parts // 2) % parts)
    return jnp.where(strong, factor * drawn, drawn)


def steps_of(key, shape, shards, low, top_value):
    def one(axis_at, shards_of):
        draws = jax.random.uniform(jax.random.fold_in(jax.random.fold_in(key, 6), axis_at), (shards_of,), jnp.float32, low / len(shards), top_value / len(shards))
        return jnp.repeat(jnp.exp(draws), shape[axis_at] // shards_of).reshape((-1,) + (1,) * (len(shape) - axis_at - 1))

    loudness = one(*shards[0])
    for cut in shards[1:]:
        loudness = loudness * one(*cut)
    return loudness


def gaussian(own_key, extent, width, limit, split=(), kind=jnp.bfloat16):
    gain = steps_of(own_key, extent, split, -0.22, 0.18) if split else 1.0
    array = jax.random.normal(own_key, extent, jnp.float32) * width * gain
    return jnp.minimum(jnp.maximum(array, -limit), limit).astype(kind)


def noise_with(own_key, extent, width, most, shards, heavy, kind=jnp.bfloat16):
    result = width * jax.random.normal(own_key, extent, jnp.float32)
    if shards:
        result = result * steps_of(own_key, extent, shards, -0.22, 0.18)
    return jnp.clip(with_spikes(result, jax.random.fold_in(own_key, 3), *heavy), -most, most).astype(kind)


def setup_inputs(seed: int = 0) -> dict:
    keys = jax.random.split(jax.random.key(seed), 7)
    field = gaussian(keys[0], (SAMPLES, WIDTH, GRID_H, GRID_W), 1.0, 6.0, ((1, 4), (2, 8)), jnp.float32)
    cotangent = gaussian(keys[1], (SAMPLES, WIDTH, GRID_H, GRID_W), 0.5, 3.0, ((1, 4), (2, 8)), jnp.float32)
    weight = noise_with(keys[2], (MODES_H, WIDTH, WIDTH, 2 * MODES_W), WIDTH ** -0.5, 0.75, ((0, 8), (1, 4)), (1, 2, 4, 2.0), jnp.float32)
    bias = gaussian(keys[3], (WIDTH,), 0.7, 3.0, (), jnp.float32)
    mode_rows = draw_mode_rows(jax.random.fold_in(keys[6], 71), 0)
    mode_cols = draw_mode_cols(jax.random.fold_in(keys[6], 71), 0)
    return dict(field=field, cotangent=cotangent, weight=weight, bias=bias, mode_rows=mode_rows, mode_cols=mode_cols)


precise_mode = lax.Precision.HIGHEST

def angle_table(modes, positions, length):
    phase = modes[:, None] * positions[None, :] % length
    return phase.astype(jnp.float32) * (2.0 * math.pi / length)

def column_table(mode_cols, length):
    angles = angle_table(mode_cols, jnp.arange(length, dtype=jnp.int32), length)
    stacked = jnp.stack([jnp.cos(angles), -jnp.sin(angles)], axis=1)
    return stacked.reshape(2 * mode_cols.shape[0], length)

def row_table(modes, positions, length):
    angles = angle_table(modes, positions, length)
    return jnp.concatenate([jnp.cos(angles), jnp.sin(angles)], axis=0)

def split_parts(values):
    shaped = values.reshape(values.shape[:-1] + (values.shape[-1] // 2, 2))
    return (shaped[..., 0], shaped[..., 1])

def join_parts(real, imag):
    return jnp.stack([real, imag], axis=-1).reshape(real.shape[:-1] + (2 * real.shape[-1],))

def analyze_rows(columns, table):
    count = table.shape[0] // 2
    shaped = columns.reshape(columns.shape[:-1] + (columns.shape[-1] // 2, 2))
    both = jnp.einsum('kh,bchmp->kbcmp', table, shaped, precision=precise_mode)
    cosine, sine = (both[:count], both[count:])
    return join_parts(cosine[..., 0] + sine[..., 1], cosine[..., 1] - sine[..., 0])

def synth_rows(modes, table):
    count = modes.shape[0]
    shaped = modes.reshape(modes.shape[:-1] + (modes.shape[-1] // 2, 2))
    cosine = jnp.einsum('kh,kbomp->bohmp', table[:count], shaped, precision=precise_mode)
    sine = jnp.einsum('kh,kbomp->bohmp', table[count:], shaped, precision=precise_mode)
    return join_parts(cosine[..., 0] - sine[..., 1], cosine[..., 1] + sine[..., 0])

def mix_modes(spectrum, weight):
    spec_re, spec_im = split_parts(spectrum)
    wgt_re, wgt_im = split_parts(weight)

    def contract(left, right):
        return jnp.einsum('kbcm,kcom->kbom', left, right, precision=precise_mode)
    real = contract(spec_re, wgt_re) - contract(spec_im, wgt_im)
    imag = contract(spec_re, wgt_im) + contract(spec_im, wgt_re)
    return join_parts(real, imag)

def mix_grads(spectrum, weight, grad_mixed):
    spec_re, spec_im = split_parts(spectrum)
    wgt_re, wgt_im = split_parts(weight)
    grad_re, grad_im = split_parts(grad_mixed)

    def outer(left, right):
        return jnp.einsum('kbom,kbcm->kcom', left, right, precision=precise_mode)

    def inner(left, right):
        return jnp.einsum('kcom,kbom->kbcm', left, right, precision=precise_mode)
    weight_re = outer(grad_re, spec_re) + outer(grad_im, spec_im)
    weight_im = outer(grad_im, spec_re) - outer(grad_re, spec_im)
    input_re = inner(wgt_re, grad_re) + inner(wgt_im, grad_im)
    input_im = inner(wgt_re, grad_im) - inner(wgt_im, grad_re)
    return (join_parts(weight_re, weight_im), join_parts(input_re, input_im))

def gelu_slope(values):
    cumulative = 0.5 * (1.0 + jax.scipy.special.erf(values / math.sqrt(2.0)))
    density = jnp.exp(-0.5 * values * values) / math.sqrt(2.0 * math.pi)
    return cumulative + values * density

def reference(field, cotangent, weight, bias, mode_rows, mode_cols):
    table_w = column_table(mode_cols, GRID_W)
    table_h = row_table(mode_rows, jnp.arange(GRID_H, dtype=jnp.int32), GRID_H)
    scale_fwd = 1.0 / math.sqrt(GRID_H * GRID_W)
    scale_inv = 1.0 / math.sqrt(MODES_H * MODES_W)
    columns = jnp.dot(field, table_w.T, precision=precise_mode, preferred_element_type=jnp.float32)
    spectrum = analyze_rows(columns, table_h) * scale_fwd
    mixed = mix_modes(spectrum, weight)
    synthesized = jnp.dot(synth_rows(mixed, table_h), table_w, precision=precise_mode, preferred_element_type=jnp.float32)
    before = synthesized * scale_inv + bias[None, :, None, None]
    grad_before = cotangent * gelu_slope(before)
    grad_columns = jnp.dot(grad_before, table_w.T, precision=precise_mode, preferred_element_type=jnp.float32)
    grad_mixed = analyze_rows(grad_columns, table_h) * scale_inv
    grad_weight, grad_spectrum = mix_grads(spectrum, weight, grad_mixed)
    grad_field = jnp.dot(synth_rows(grad_spectrum, table_h), table_w, precision=precise_mode, preferred_element_type=jnp.float32) * scale_fwd
    return (grad_field, grad_weight)
```

```python
import functools
import math

import jax
import jax.numpy as jnp
from jax import lax
from jax.experimental import pallas as pl
from jax.experimental.pallas import tpu as pltpu
from jax.sharding import PartitionSpec as P

precise_mode = lax.Precision.HIGHEST


def angle_table(modes, positions, length):
    phase = modes[:, None] * positions[None, :] % length
    return phase.astype(jnp.float32) * (2.0 * math.pi / length)


def column_table(mode_cols, length):
    angles = angle_table(mode_cols, jnp.arange(length, dtype=jnp.int32), length)
    stacked = jnp.stack([jnp.cos(angles), -jnp.sin(angles)], axis=1)
    return stacked.reshape(2 * mode_cols.shape[0], length)


def row_table(modes, positions, length):
    angles = angle_table(modes, positions, length)
    return jnp.concatenate([jnp.cos(angles), jnp.sin(angles)], axis=0)


def split_parts(values):
    shaped = values.reshape(values.shape[:-1] + (values.shape[-1] // 2, 2))
    return (shaped[..., 0], shaped[..., 1])


def join_parts(real, imag):
    return jnp.stack([real, imag], axis=-1).reshape(real.shape[:-1] + (2 * real.shape[-1],))


def analyze_rows(columns, table):
    count = table.shape[0] // 2
    shaped = columns.reshape(columns.shape[:-1] + (columns.shape[-1] // 2, 2))
    both = jnp.einsum("kh,bchmp->kbcmp", table, shaped, precision=precise_mode)
    cosine, sine = (both[:count], both[count:])
    return join_parts(cosine[..., 0] + sine[..., 1], cosine[..., 1] - sine[..., 0])


def synth_rows(modes, table):
    count = modes.shape[0]
    shaped = modes.reshape(modes.shape[:-1] + (modes.shape[-1] // 2, 2))
    cosine = jnp.einsum("kh,kbomp->bohmp", table[:count], shaped, precision=precise_mode)
    sine = jnp.einsum("kh,kbomp->bohmp", table[count:], shaped, precision=precise_mode)
    return join_parts(cosine[..., 0] - sine[..., 1], cosine[..., 1] + sine[..., 0])


def mix_modes(spectrum, weight):
    spec_re, spec_im = split_parts(spectrum)
    wgt_re, wgt_im = split_parts(weight)

    def contract(left, right):
        return jnp.einsum("kbcm,kcom->kbom", left, right, precision=precise_mode)

    real = contract(spec_re, wgt_re) - contract(spec_im, wgt_im)
    imag = contract(spec_re, wgt_im) + contract(spec_im, wgt_re)
    return join_parts(real, imag)


def mix_grads(spectrum, weight, grad_mixed):
    spec_re, spec_im = split_parts(spectrum)
    wgt_re, wgt_im = split_parts(weight)
    grad_re, grad_im = split_parts(grad_mixed)

    def outer(left, right):
        return jnp.einsum("kbom,kbcm->kcom", left, right, precision=precise_mode)

    def inner(left, right):
        return jnp.einsum("kcom,kbom->kbcm", left, right, precision=precise_mode)

    weight_re = outer(grad_re, spec_re) + outer(grad_im, spec_im)
    weight_im = outer(grad_im, spec_re) - outer(grad_re, spec_im)
    input_re = inner(wgt_re, grad_re) + inner(wgt_im, grad_im)
    input_im = inner(wgt_re, grad_im) - inner(wgt_im, grad_re)
    return (join_parts(weight_re, weight_im), join_parts(input_re, input_im))


def gelu_slope(values):
    cumulative = 0.5 * (1.0 + jax.scipy.special.erf(values / math.sqrt(2.0)))
    density = jnp.exp(-0.5 * values * values) / math.sqrt(2.0 * math.pi)
    return cumulative + values * density


def body(field, cotangent, weight, bias, mode_rows, mode_cols):
    rows_here = field.shape[2]
    row_count = lax.axis_size("rows")
    grid_rows = rows_here * row_count
    grid_cols = field.shape[3]
    all_rows = jnp.arange(grid_rows, dtype=jnp.int32)
    table_w = column_table(mode_cols, grid_cols)
    scale_fwd = 1.0 / math.sqrt(grid_rows * grid_cols)
    scale_inv = 1.0 / math.sqrt(mode_rows.shape[0] * mode_cols.shape[0])

    def analyze(values):
        columns = jnp.dot(
            values, table_w.T, precision=precise_mode, preferred_element_type=jnp.float32
        )
        spread = lax.all_to_all(columns, "rows", split_axis=3, concat_axis=2, tiled=True)
        pieces = analyze_rows(spread, row_table(mode_rows, all_rows, grid_rows))
        return lax.all_to_all(pieces, "rows", split_axis=0, concat_axis=3, tiled=True)

    def synthesize(modes):
        spread = lax.all_to_all(modes, "rows", split_axis=3, concat_axis=0, tiled=True)
        pieces = synth_rows(spread, row_table(mode_rows, all_rows, grid_rows))
        gathered = lax.all_to_all(pieces, "rows", split_axis=2, concat_axis=3, tiled=True)
        return jnp.dot(
            gathered, table_w, precision=precise_mode, preferred_element_type=jnp.float32
        )

    spectrum = analyze(field) * scale_fwd
    mixed = lax.psum_scatter(mix_modes(spectrum, weight), "ch", scatter_dimension=2, tiled=True)
    outputs_here = mixed.shape[2]
    bias_here = lax.dynamic_slice_in_dim(bias, lax.axis_index("ch") * outputs_here, outputs_here)
    before = synthesize(mixed) * scale_inv + bias_here[None, :, None, None]
    grad_before = cotangent * gelu_slope(before)
    grad_mixed = analyze(grad_before) * scale_inv
    grad_whole = lax.all_gather(grad_mixed, "ch", axis=2, tiled=True)
    grad_weight, grad_spectrum = mix_grads(spectrum, weight, grad_whole)
    grad_field = synthesize(grad_spectrum) * scale_fwd
    return (grad_field, grad_weight)


def split_bf16(values):
    high = values.astype(jnp.bfloat16)
    low = (values - high.astype(jnp.float32)).astype(jnp.bfloat16)
    return high, low


def turn_cosine(step, length):
    step = lax.rem(step, jnp.int32(length)) if length & (length - 1) else step & (length - 1)
    folded = jnp.abs(step - length // 2) - length // 4
    angle = folded.astype(jnp.float32) * (2.0 * math.pi / length)
    square = angle * angle
    total = jnp.float32(-2.5052108e-08)
    for factor in (2.7557319e-06, -1.9841270e-04, 8.3333333e-03, -1.6666667e-01):
        total = total * square + factor
    return angle + angle * square * total


def next_lane(values):
    return pltpu.roll(values, values.shape[-1] - 1, values.ndim - 1)


def prev_lane(values):
    return pltpu.roll(values, 1, values.ndim - 1)


def even_lanes(values):
    return lax.broadcasted_iota(jnp.int32, values.shape, values.ndim - 1) % 2 == 0


def swap_pairs(values):
    return jnp.where(even_lanes(values), next_lane(values), prev_lane(values))


def layer_kernel(
    sizes, field_ref, cot_hbm, weight_hbm, bias_ref, colmode_ref, rowmode_ref, rowlane_ref,
    gfield_ref, same_ref, cross_ref, grads_ref,
    weight_ref, cot_ref, high_ref, low_ref, fwd_ref, inv_ref, flat_ref, stack_ref,
    four_ref, many_ref, part_ref, arrive_ref, gall_ref, gswap_ref, accp_ref, accq_ref,
    local_sem, send_sem, recv_sem, ch_send, ch_recv,
):
    samples, chans, rows_here, width, kept, ranks, groups, lanes = sizes
    grid_rows = rows_here * ranks
    kept_here = kept // ranks
    pairs = samples * chans
    own_pairs = pairs // ranks
    flat_rows = pairs * rows_here
    scale_fwd = 1.0 / math.sqrt(grid_rows * width)
    scale_inv = 1.0 / math.sqrt(kept * (lanes // 2))
    me, mine = lax.axis_index("rows"), lax.axis_index("ch")
    mesh_ids = pl.DeviceIdType.MESH

    def rank_at(step):
        return lax.rem(me + step, ranks)

    def group_at(step):
        return lax.rem(mine + step, groups)

    barrier = pltpu.get_barrier_semaphore()
    for step in range(1, ranks):
        pl.semaphore_signal(barrier, inc=1, device_id=(rank_at(step), mine), device_id_type=mesh_ids)
    for step in range(1, groups):
        pl.semaphore_signal(barrier, inc=1, device_id=(me, group_at(step)), device_id_type=mesh_ids)

    load_weight = pltpu.make_async_copy(weight_hbm, weight_ref, local_sem.at[0])
    load_weight.start()
    load_cot = pltpu.make_async_copy(cot_hbm, cot_ref, local_sem.at[1])
    load_cot.start()

    chunk = 128

    @pl.loop(0, width // chunk)
    def _(at):
        shape = (chunk, lanes)
        column = lax.broadcasted_iota(jnp.int32, shape, 0) + at * chunk
        quarter = lax.broadcasted_iota(jnp.int32, shape, 1) % 2 * (width // 4)
        high, low = split_bf16(turn_cosine(colmode_ref[...] * column + quarter, width))
        here = pl.ds(pl.multiple_of(at * chunk, chunk), chunk)
        high_ref[here, :] = high
        low_ref[here, :] = low

    def packed_table(step, length):
        table = turn_cosine(step, length)
        high, low = split_bf16(table)
        lane = lax.broadcasted_iota(jnp.int32, table.shape, 1)
        edge = table.shape[1] // 3 * 2
        chosen = jnp.where(lane < edge, high.astype(jnp.float32), low.astype(jnp.float32))
        return chosen.astype(jnp.bfloat16)

    spot = lax.broadcasted_iota(jnp.int32, (kept, 6 * grid_rows), 1)
    turn = spot // grid_rows % 2 * (3 * grid_rows // 4)
    fwd_ref[...] = packed_table(rowmode_ref[...] * (spot % grid_rows) + turn, grid_rows)
    spot = lax.broadcasted_iota(jnp.int32, (grid_rows, 6 * kept), 1)
    turn = spot // kept % 2 * (grid_rows // 4)
    row = lax.broadcasted_iota(jnp.int32, (grid_rows, 6 * kept), 0)
    inv_ref[...] = packed_table(rowlane_ref[...] * row + turn, grid_rows)

    def analyze_cols(values):
        high, low = split_bf16(values)
        dims = (((1,), (0,)), ((), ()))

        def product(left, right):
            return lax.dot_general(left, right, dims, preferred_element_type=jnp.float32)

        return (
            product(high, low_ref[...]) + product(low, high_ref[...]) + product(high, high_ref[...])
        )

    def synth_cols(values):
        high, low = split_bf16(values)
        dims = (((1,), (1,)), ((), ()))

        def product(left, right):
            return lax.dot_general(left, right, dims, preferred_element_type=jnp.float32)

        return (
            product(high, low_ref[...]) + product(low, high_ref[...]) + product(high, high_ref[...])
        )

    def to_rows(out_ref):
        for h in range(rows_here):
            out_ref[h] = flat_ref[pl.ds(h, pairs, stride=rows_here), :]

    def from_rows(in_ref):
        for h in range(rows_here):
            flat_ref[pl.ds(h, pairs, stride=rows_here), :] = in_ref[h]

    def block(rank, size):
        return pl.ds(pl.multiple_of(rank * size, size), size)

    def exchange(phase, source, target, slab):
        copies = []
        for step in range(1, ranks):
            peer = rank_at(step)
            copy = pltpu.make_async_remote_copy(
                src_ref=source(peer), dst_ref=target(me),
                send_sem=send_sem.at[phase, step - 1], recv_sem=recv_sem.at[phase, step - 1],
                device_id=(peer, mine), device_id_type=mesh_ids,
            )
            copy.start()
            copies.append(copy)
        target(me)[...] = source(me)[...]
        for copy in copies:
            copy.wait_recv()
        return copies

    sent = []

    def spread(phase, few, many):
        size = few.shape[0]
        sent.extend(exchange(
            phase,
            lambda rank: few.at[:, block(rank, own_pairs), :],
            lambda rank: many.at[block(rank, size)],
            size,
        ))

    def collect(phase, many, few):
        size = few.shape[0]
        sent.extend(exchange(
            phase,
            lambda rank: many.at[block(rank, size)],
            lambda rank: few.at[:, block(rank, own_pairs), :],
            size,
        ))

    def transform_rows(table_ref, in_ref, out_ref, scale):
        count = in_ref.shape[0]
        for pair in range(own_pairs):
            values = in_ref[:, pair, :]
            crossed = jnp.where(even_lanes(values), next_lane(values), -prev_lane(values))
            here = slice(pair * lanes, (pair + 1) * lanes)
            for at, piece in enumerate((values, crossed)):
                high, low = split_bf16(piece)
                stack_ref[at * count:(at + 1) * count, here] = high
                stack_ref[(2 + at) * count:(3 + at) * count, here] = low
                stack_ref[(4 + at) * count:(5 + at) * count, here] = high
        result = jnp.dot(
            table_ref[...], stack_ref[...], preferred_element_type=jnp.float32
        )
        if scale is not None:
            result = result * scale
        for pair in range(own_pairs):
            out_ref[:, pair, :] = result[:, pair * lanes:(pair + 1) * lanes]

    flat_ref[...] = analyze_cols(field_ref[...])
    to_rows(four_ref.at[0])
    pl.semaphore_wait(barrier, ranks - 1 + groups - 1)
    spread(0, four_ref.at[0], many_ref.at[0])
    transform_rows(fwd_ref, many_ref.at[0], many_ref.at[1], scale_fwd)
    collect(1, many_ref.at[1], four_ref.at[1])

    spectrum = four_ref.at[1]
    for k in range(kept_here):
        values = spectrum[k]
        even = even_lanes(values)
        same_ref[k] = jnp.where(even, values, prev_lane(values))
        cross_ref[k] = jnp.where(even, next_lane(values), -values)

    load_weight.wait()

    def mix_group(group, out_ref):
        outs = pl.ds(pl.multiple_of(group * chans, chans), chans)

        @pl.loop(0, kept_here)
        def _(k):
            plain = [jnp.zeros((chans, lanes), jnp.float32) for _ in range(samples)]
            turned = [jnp.zeros((chans, lanes), jnp.float32) for _ in range(samples)]
            for c in range(chans):
                w = weight_ref[k, c, outs, :]
                for b in range(samples):
                    at = b * chans + c
                    plain[b] = plain[b] + w * same_ref[k, at:at + 1, :]
                    turned[b] = turned[b] + w * cross_ref[k, at:at + 1, :]
            for b in range(samples):
                out_ref[k, b * chans:(b + 1) * chans, :] = plain[b] + swap_pairs(turned[b])

    order = sorted(range(1, groups), key=lambda step: -min(step, groups - step))
    sums = []
    for step in order:
        mix_group(group_at(step), part_ref.at[step - 1])
        copy = pltpu.make_async_remote_copy(
            src_ref=part_ref.at[step - 1], dst_ref=arrive_ref.at[step - 1],
            send_sem=ch_send.at[0, step - 1], recv_sem=ch_recv.at[0, step - 1],
            device_id=(me, group_at(step)), device_id_type=mesh_ids,
        )
        copy.start()
        sums.append(copy)
    mixed = four_ref.at[2]
    mix_group(mine, mixed)
    for copy in sums:
        copy.wait_recv()
    sent.extend(sums)
    for k in range(kept_here):
        total = mixed[k]
        for step in order:
            total = total + arrive_ref[step - 1, k]
        mixed[k] = total

    spread(2, mixed, many_ref.at[2])
    transform_rows(inv_ref, many_ref.at[2], many_ref.at[3], scale_inv)
    collect(3, many_ref.at[3], four_ref.at[3])
    from_rows(four_ref.at[3])

    whole = bias_ref.shape[1]
    out_chan = mine * chans + lax.broadcasted_iota(jnp.int32, (flat_rows, whole), 0) // rows_here % chans
    picked = lax.broadcasted_iota(jnp.int32, (flat_rows, whole), 1) == out_chan
    bias_rows = jnp.sum(jnp.where(picked, bias_ref[...], 0.0), axis=1, keepdims=True)
    load_cot.wait()
    before = synth_cols(flat_ref[...]) + bias_rows
    slope = 0.5 * (1.0 + lax.erf(before * (1.0 / math.sqrt(2.0))))
    slope = slope + before * jnp.exp(-0.5 * before * before) * (1.0 / math.sqrt(2.0 * math.pi))
    flat_ref[...] = analyze_cols(cot_ref[...] * slope)
    to_rows(four_ref.at[4])
    spread(4, four_ref.at[4], many_ref.at[4])
    transform_rows(fwd_ref, many_ref.at[4], many_ref.at[5], scale_inv)
    collect(5, many_ref.at[5], four_ref.at[5])

    own = four_ref.at[5]
    gathers = []
    for step in order:
        copy = pltpu.make_async_remote_copy(
            src_ref=own, dst_ref=gall_ref.at[mine],
            send_sem=ch_send.at[1, step - 1], recv_sem=ch_recv.at[1, step - 1],
            device_id=(me, group_at(step)), device_id_type=mesh_ids,
        )
        copy.start()
        gathers.append((step, copy))
    sent.extend(copy for _, copy in gathers)

    accp_ref[...] = jnp.zeros_like(accp_ref)
    accq_ref[...] = jnp.zeros_like(accq_ref)
    tile = 8

    def back_group(group, grad_ref):
        for k in range(kept_here):
            gswap_ref[k] = swap_pairs(grad_ref[k])

        @pl.loop(0, kept_here * (chans // tile))
        def _(at):
            k, first = at // (chans // tile), at % (chans // tile) * tile
            sums = [[None] * (2 * samples) for _ in range(tile)]
            for o in range(0, chans, tile):
                factors = []
                for b in range(samples):
                    factors.append(grad_ref[k, b * chans + o:b * chans + o + tile, :])
                    factors.append(gswap_ref[k, b * chans + o:b * chans + o + tile, :])
                outs = pl.ds(pl.multiple_of(group * chans + o, tile), tile)
                for c in range(tile):
                    w = weight_ref[k, first + c, outs, :]
                    for i, factor in enumerate(factors):
                        term = w * factor
                        sums[c][i] = term if sums[c][i] is None else sums[c][i] + term
            for b in range(samples):
                here = pl.ds(pl.multiple_of(b * chans + first, tile), tile)
                for i, acc_ref in ((2 * b, accp_ref), (2 * b + 1, accq_ref)):
                    rows = [jnp.sum(sums[c][i], axis=0, keepdims=True) for c in range(tile)]
                    acc_ref[k, here, :] += jnp.concatenate(rows, axis=0)

    back_group(mine, own)
    for step, copy in sorted(gathers, key=lambda pair: min(pair[0], groups - pair[0])):
        copy.wait_recv()
        source = lax.rem(mine + groups - step, groups)
        back_group(source, gall_ref.at[source])
    gspec = four_ref.at[6]
    for k in range(kept_here):
        p, q = accp_ref[k], accq_ref[k]
        gspec[k] = jnp.where(even_lanes(p), p + next_lane(p), prev_lane(q) - q)

    spread(6, gspec, many_ref.at[6])
    transform_rows(inv_ref, many_ref.at[6], many_ref.at[7], scale_fwd)
    collect(7, many_ref.at[7], four_ref.at[7])
    from_rows(four_ref.at[7])
    gfield_ref[...] = synth_cols(flat_ref[...])
    for step in range(1, groups):
        grads_ref[group_at(step)] = gall_ref[group_at(step)]
    grads_ref[mine] = own[...]
    for copy in sent:
        copy.wait_send()


def weight_kernel(chans, samples, same_ref, cross_ref, grads_ref, out_ref):
    tile = 8
    first = pl.multiple_of(pl.program_id(1) * out_ref.shape[1], tile)
    count = out_ref.shape[1]
    same = [same_ref[0, pl.ds(b * chans + first, count), :] for b in range(samples)]
    cross = [cross_ref[0, pl.ds(b * chans + first, count), :] for b in range(samples)]
    for group in range(grads_ref.shape[0]):
        for o in range(0, chans, tile):
            plain = [grads_ref[group, 0, b * chans + o:b * chans + o + tile, :] for b in range(samples)]
            turned = [swap_pairs(values) for values in plain]
            at = group * chans + o
            for c in range(count):
                total = plain[0] * same[0][c:c + 1] + turned[0] * cross[0][c:c + 1]
                for b in range(1, samples):
                    total = total + plain[b] * same[b][c:c + 1] + turned[b] * cross[b][c:c + 1]
                out_ref[0, c, at:at + tile, :] = total


def kernel_fits(ranks, groups, field, weight, mode_rows, bias):
    pairs = field.shape[0] * field.shape[1]
    lanes = weight.shape[3]
    return (
        pairs % (8 * ranks) == 0 and lanes == 128 and field.shape[1] % 8 == 0
        and field.shape[1] * groups == weight.shape[2] and mode_rows.shape[0] % 32 == 0
        and field.shape[2] * ranks % 32 == 0 and mode_rows.shape[0] == field.shape[2] * ranks
        and field.shape[3] % 128 == 0 and bias.shape[0] % 128 == 0
    )


def kernel_body(field, cotangent, weight, bias, mode_rows, mode_cols):
    samples, chans, rows_here, width = field.shape
    ranks, groups = lax.axis_size("rows"), lax.axis_size("ch")
    kept, lanes = mode_rows.shape[0], weight.shape[3]
    grid_rows = rows_here * ranks
    kept_here = kept // ranks
    pairs = samples * chans
    own_pairs = pairs // ranks
    flat_rows = pairs * rows_here
    f32, bf16 = jnp.float32, jnp.bfloat16
    sizes = (samples, chans, rows_here, width, kept, ranks, groups, lanes)
    vmem = pl.BlockSpec(memory_space=pltpu.VMEM)
    hbm = pl.BlockSpec(memory_space=pl.ANY)
    modes = (kept_here, pairs, lanes)
    dma = pltpu.SemaphoreType.DMA
    gfield, same, cross, grads = pl.pallas_call(
        functools.partial(layer_kernel, sizes),
        out_shape=(
            jax.ShapeDtypeStruct((flat_rows, width), f32),
            jax.ShapeDtypeStruct(modes, f32),
            jax.ShapeDtypeStruct(modes, f32),
            jax.ShapeDtypeStruct((groups,) + modes, f32),
        ),
        in_specs=[vmem, hbm, hbm, vmem, vmem, vmem, vmem],
        out_specs=(vmem,) * 4,
        scratch_shapes=[
            pltpu.VMEM(weight.shape, f32),
            pltpu.VMEM((flat_rows, width), f32),
            pltpu.VMEM((width, lanes), bf16),
            pltpu.VMEM((width, lanes), bf16),
            pltpu.VMEM((kept, 6 * grid_rows), bf16),
            pltpu.VMEM((grid_rows, 6 * kept), bf16),
            pltpu.VMEM((flat_rows, lanes), f32),
            pltpu.VMEM((6 * kept, own_pairs * lanes), bf16),
            pltpu.VMEM((8,) + modes, f32),
            pltpu.VMEM((8, grid_rows, own_pairs, lanes), f32),
            pltpu.VMEM((groups - 1,) + modes, f32),
            pltpu.VMEM((groups - 1,) + modes, f32),
            pltpu.VMEM((groups,) + modes, f32),
            pltpu.VMEM(modes, f32),
            pltpu.VMEM(modes, f32),
            pltpu.VMEM(modes, f32),
            dma((2,)),
            dma((8, ranks - 1)),
            dma((8, ranks - 1)),
            dma((2, groups - 1)),
            dma((2, groups - 1)),
        ],
        compiler_params=pltpu.CompilerParams(
            collective_id=0, has_side_effects=True, vmem_limit_bytes=52 * 1024 * 1024
        ),
    )(
        field.reshape(flat_rows, width),
        cotangent.reshape(flat_rows, width),
        weight,
        bias.reshape(1, bias.shape[0]),
        jnp.repeat(mode_cols, 2).reshape(1, lanes),
        mode_rows.reshape(kept, 1),
        jnp.tile(mode_rows, 6).reshape(1, 6 * kept),
    )
    count = 8
    one = pl.BlockSpec((1, pairs, lanes), lambda k, c: (k, 0, 0))
    gweight = pl.pallas_call(
        functools.partial(weight_kernel, chans, samples),
        out_shape=jax.ShapeDtypeStruct(weight.shape, f32),
        grid=(kept_here, chans // count),
        in_specs=[one, one, pl.BlockSpec((groups, 1, pairs, lanes), lambda k, c: (0, k, 0, 0))],
        out_specs=pl.BlockSpec((1, count) + weight.shape[2:], lambda k, c: (k, c, 0, 0)),
        compiler_params=pltpu.CompilerParams(vmem_limit_bytes=32 * 1024 * 1024),
    )(same, cross, grads)
    return gfield.reshape(field.shape), gweight


def any_body(field, cotangent, weight, bias, mode_rows, mode_cols):
    ranks, groups = lax.axis_size("rows"), lax.axis_size("ch")
    chosen = kernel_body if kernel_fits(ranks, groups, field, weight, mode_rows, bias) else body
    return chosen(field, cotangent, weight, bias, mode_rows, mode_cols)


def solution(mesh):
    return jax.shard_map(
        any_body,
        mesh=mesh,
        in_specs=(
            P(None, "ch", "rows", None),
            P(None, "ch", "rows", None),
            P("rows", "ch", None, None),
            P(),
            P(),
            P(),
        ),
        out_specs=(P(None, "ch", "rows", None), P("rows", "ch", None, None)),
        check_vma=False,
    )
```

```python
import functools
import math

import jax
import jax.numpy as jnp
from jax import lax
from jax.experimental import pallas as pl
from jax.experimental.pallas import tpu as pltpu
from jax.sharding import PartitionSpec as P

precise_mode = lax.Precision.HIGHEST


def angle_table(modes, positions, length):
    phase = modes[:, None] * positions[None, :] % length
    return phase.astype(jnp.float32) * (2.0 * math.pi / length)


def column_table(mode_cols, length):
    angles = angle_table(mode_cols, jnp.arange(length, dtype=jnp.int32), length)
    stacked = jnp.stack([jnp.cos(angles), -jnp.sin(angles)], axis=1)
    return stacked.reshape(2 * mode_cols.shape[0], length)


def row_table(modes, positions, length):
    angles = angle_table(modes, positions, length)
    return jnp.concatenate([jnp.cos(angles), jnp.sin(angles)], axis=0)


def split_parts(values):
    shaped = values.reshape(values.shape[:-1] + (values.shape[-1] // 2, 2))
    return (shaped[..., 0], shaped[..., 1])


def join_parts(real, imag):
    return jnp.stack([real, imag], axis=-1).reshape(real.shape[:-1] + (2 * real.shape[-1],))


def analyze_rows(columns, table):
    count = table.shape[0] // 2
    shaped = columns.reshape(columns.shape[:-1] + (columns.shape[-1] // 2, 2))
    both = jnp.einsum("kh,bchmp->kbcmp", table, shaped, precision=precise_mode)
    cosine, sine = (both[:count], both[count:])
    return join_parts(cosine[..., 0] + sine[..., 1], cosine[..., 1] - sine[..., 0])


def synth_rows(modes, table):
    count = modes.shape[0]
    shaped = modes.reshape(modes.shape[:-1] + (modes.shape[-1] // 2, 2))
    cosine = jnp.einsum("kh,kbomp->bohmp", table[:count], shaped, precision=precise_mode)
    sine = jnp.einsum("kh,kbomp->bohmp", table[count:], shaped, precision=precise_mode)
    return join_parts(cosine[..., 0] - sine[..., 1], cosine[..., 1] + sine[..., 0])


def mix_modes(spectrum, weight):
    spec_re, spec_im = split_parts(spectrum)
    wgt_re, wgt_im = split_parts(weight)

    def contract(left, right):
        return jnp.einsum("kbcm,kcom->kbom", left, right, precision=precise_mode)

    real = contract(spec_re, wgt_re) - contract(spec_im, wgt_im)
    imag = contract(spec_re, wgt_im) + contract(spec_im, wgt_re)
    return join_parts(real, imag)


def mix_grads(spectrum, weight, grad_mixed):
    spec_re, spec_im = split_parts(spectrum)
    wgt_re, wgt_im = split_parts(weight)
    grad_re, grad_im = split_parts(grad_mixed)

    def outer(left, right):
        return jnp.einsum("kbom,kbcm->kcom", left, right, precision=precise_mode)

    def inner(left, right):
        return jnp.einsum("kcom,kbom->kbcm", left, right, precision=precise_mode)

    weight_re = outer(grad_re, spec_re) + outer(grad_im, spec_im)
    weight_im = outer(grad_im, spec_re) - outer(grad_re, spec_im)
    input_re = inner(wgt_re, grad_re) + inner(wgt_im, grad_im)
    input_im = inner(wgt_re, grad_im) - inner(wgt_im, grad_re)
    return (join_parts(weight_re, weight_im), join_parts(input_re, input_im))


def gelu_slope(values):
    cumulative = 0.5 * (1.0 + jax.scipy.special.erf(values / math.sqrt(2.0)))
    density = jnp.exp(-0.5 * values * values) / math.sqrt(2.0 * math.pi)
    return cumulative + values * density


def body(field, cotangent, weight, bias, mode_rows, mode_cols):
    rows_here = field.shape[2]
    row_count = lax.axis_size("rows")
    grid_rows = rows_here * row_count
    grid_cols = field.shape[3]
    all_rows = jnp.arange(grid_rows, dtype=jnp.int32)
    table_w = column_table(mode_cols, grid_cols)
    scale_fwd = 1.0 / math.sqrt(grid_rows * grid_cols)
    scale_inv = 1.0 / math.sqrt(mode_rows.shape[0] * mode_cols.shape[0])

    def analyze(values):
        columns = jnp.dot(
            values, table_w.T, precision=precise_mode, preferred_element_type=jnp.float32
        )
        spread = lax.all_to_all(columns, "rows", split_axis=3, concat_axis=2, tiled=True)
        pieces = analyze_rows(spread, row_table(mode_rows, all_rows, grid_rows))
        return lax.all_to_all(pieces, "rows", split_axis=0, concat_axis=3, tiled=True)

    def synthesize(modes):
        spread = lax.all_to_all(modes, "rows", split_axis=3, concat_axis=0, tiled=True)
        pieces = synth_rows(spread, row_table(mode_rows, all_rows, grid_rows))
        gathered = lax.all_to_all(pieces, "rows", split_axis=2, concat_axis=3, tiled=True)
        return jnp.dot(
            gathered, table_w, precision=precise_mode, preferred_element_type=jnp.float32
        )

    spectrum = analyze(field) * scale_fwd
    mixed = lax.psum_scatter(mix_modes(spectrum, weight), "ch", scatter_dimension=2, tiled=True)
    outputs_here = mixed.shape[2]
    bias_here = lax.dynamic_slice_in_dim(bias, lax.axis_index("ch") * outputs_here, outputs_here)
    before = synthesize(mixed) * scale_inv + bias_here[None, :, None, None]
    grad_before = cotangent * gelu_slope(before)
    grad_mixed = analyze(grad_before) * scale_inv
    grad_whole = lax.all_gather(grad_mixed, "ch", axis=2, tiled=True)
    grad_weight, grad_spectrum = mix_grads(spectrum, weight, grad_whole)
    grad_field = synthesize(grad_spectrum) * scale_fwd
    return (grad_field, grad_weight)


def split_bf16(values):
    high = values.astype(jnp.bfloat16)
    low = (values - high.astype(jnp.float32)).astype(jnp.bfloat16)
    return high, low


def turn_cosine(step, length):
    step = lax.rem(step, jnp.int32(length)) if length & (length - 1) else step & (length - 1)
    folded = jnp.abs(step - length // 2) - length // 4
    angle = folded.astype(jnp.float32) * (2.0 * math.pi / length)
    square = angle * angle
    total = jnp.float32(-2.5052108e-08)
    for factor in (2.7557319e-06, -1.9841270e-04, 8.3333333e-03, -1.6666667e-01):
        total = total * square + factor
    return angle + angle * square * total


def next_lane(values):
    return pltpu.roll(values, values.shape[-1] - 1, values.ndim - 1)


def prev_lane(values):
    return pltpu.roll(values, 1, values.ndim - 1)


def even_lanes(values):
    return lax.broadcasted_iota(jnp.int32, values.shape, values.ndim - 1) % 2 == 0


def swap_pairs(values):
    return jnp.where(even_lanes(values), next_lane(values), prev_lane(values))


def layer_kernel(
    sizes, field_hbm, cot_hbm, weight_hbm, bias_hbm, colmode_hbm, rowmode_hbm,
    gfield_hbm, same_ref, cross_ref, grads_ref, gswap_ref,
    weight_ref, field_ref, cot_ref, gfield_ref, bias_ref, colmode_ref, rowmode_ref,
    high_ref, low_ref, fwd_ref, inv_ref, stack_ref,
    few_ref, many_ref, part_ref, arrive_ref, gall_ref, accp_ref, accq_ref,
    local_sem, field_sem, send_sem, recv_sem, ch_send, ch_recv,
):
    samples, chans, rows_here, width, kept, ranks, groups, lanes = sizes
    grid_rows = rows_here * ranks
    kept_here = kept // ranks
    handlers = ranks // samples
    own_chans = chans // handlers
    flat_rows = chans * rows_here
    scale_fwd = 1.0 / math.sqrt(grid_rows * width)
    scale_inv = 1.0 / math.sqrt(kept * (lanes // 2))
    me, mine = lax.axis_index("rows"), lax.axis_index("ch")
    my_sample, my_slot = lax.rem(me, samples), me // samples
    mesh_ids = pl.DeviceIdType.MESH

    def rank_at(step):
        return lax.rem(me + step, ranks)

    def group_at(step):
        return lax.rem(mine + step, groups)

    barrier = pltpu.get_barrier_semaphore()
    for step in range(1, ranks):
        pl.semaphore_signal(barrier, inc=1, device_id=(rank_at(step), mine), device_id_type=mesh_ids)
    for step in range(1, groups):
        pl.semaphore_signal(barrier, inc=1, device_id=(me, group_at(step)), device_id_type=mesh_ids)

    loads = []
    for at, (source, target) in enumerate((
        (colmode_hbm, colmode_ref), (rowmode_hbm, rowmode_ref), (bias_hbm, bias_ref),
    )):
        load = pltpu.make_async_copy(source, target, local_sem.at[at])
        load.start()
        loads.append(load)

    def row_copies(source, target, kind):
        found = []
        for b in range(samples):
            for h in range(rows_here):
                copy = pltpu.make_async_copy(
                    source.at[b, :, h, :], target.at[b, h], field_sem.at[kind, b, h]
                )
                copy.start()
                found.append(copy)
        return found

    load_field = row_copies(field_hbm, field_ref, 0)
    load_weight = pltpu.make_async_copy(weight_hbm, weight_ref, local_sem.at[3])
    load_weight.start()
    load_cot = row_copies(cot_hbm, cot_ref, 1)
    for load in loads:
        load.wait()

    def as_column(values):
        count = values.shape[1]
        row = lax.broadcasted_iota(jnp.int32, (count, count), 0)
        lane = lax.broadcasted_iota(jnp.int32, (count, count), 1)
        kept_values = jnp.where(row == lane, values.astype(jnp.float32), 0.0)
        return jnp.sum(kept_values, axis=1, keepdims=True)

    def pick(column, index):
        row = lax.broadcasted_iota(jnp.int32, (column.shape[0], index.shape[1]), 0)
        return jnp.sum(jnp.where(row == index, column, 0.0), axis=0, keepdims=True).astype(jnp.int32)

    col_column = as_column(colmode_ref[...])
    col_lanes = pick(col_column, lax.broadcasted_iota(jnp.int32, (1, lanes), 1) // 2)
    row_column = as_column(rowmode_ref[...])
    row_lanes = pick(row_column, lax.broadcasted_iota(jnp.int32, (1, 6 * kept), 1) % kept)
    row_column = row_column.astype(jnp.int32)
    chunk = 128

    @pl.loop(0, width // chunk)
    def _(at):
        shape = (chunk, lanes)
        column = lax.broadcasted_iota(jnp.int32, shape, 0) + at * chunk
        quarter = lax.broadcasted_iota(jnp.int32, shape, 1) % 2 * (width // 4)
        high, low = split_bf16(turn_cosine(col_lanes * column + quarter, width))
        here = pl.ds(pl.multiple_of(at * chunk, chunk), chunk)
        high_ref[here, :] = high
        low_ref[here, :] = low

    def packed_table(step, length):
        table = turn_cosine(step, length)
        high, low = split_bf16(table)
        lane = lax.broadcasted_iota(jnp.int32, table.shape, 1)
        edge = table.shape[1] // 3 * 2
        chosen = jnp.where(lane < edge, high.astype(jnp.float32), low.astype(jnp.float32))
        return chosen.astype(jnp.bfloat16)

    spot = lax.broadcasted_iota(jnp.int32, (kept, 6 * grid_rows), 1)
    turn = spot // grid_rows % 2 * (3 * grid_rows // 4)
    fwd_ref[...] = packed_table(row_column * (spot % grid_rows) + turn, grid_rows)
    spot = lax.broadcasted_iota(jnp.int32, (grid_rows, 6 * kept), 1)
    turn = spot // kept % 2 * (grid_rows // 4)
    row = lax.broadcasted_iota(jnp.int32, (grid_rows, 6 * kept), 0)
    inv_ref[...] = packed_table(row_lanes * row + turn, grid_rows)
    whole = bias_ref.shape[1]
    out_chan = mine * chans + lax.broadcasted_iota(jnp.int32, (flat_rows, whole), 0) % chans
    picked = lax.broadcasted_iota(jnp.int32, (flat_rows, whole), 1) == out_chan
    bias_rows = jnp.sum(jnp.where(picked, bias_ref[...], 0.0), axis=1, keepdims=True)

    def column_product(values, contract):
        high, low = split_bf16(values)
        dims = (((1,), (contract,)), ((), ()))

        def product(left, right):
            return lax.dot_general(left, right, dims, preferred_element_type=jnp.float32)

        return (
            product(high, low_ref[...]) + product(low, high_ref[...]) + product(high, high_ref[...])
        )

    def analyze_cols(values):
        result = column_product(values.reshape(flat_rows, width), 0)
        return result.reshape(rows_here, chans, lanes)

    def synth_cols(values):
        return column_product(values.reshape(flat_rows, lanes), 1)

    def block(rank, size):
        return pl.ds(pl.multiple_of(rank * size, size), size)

    def row_copy(phase, source, target, peer, origin):
        return pltpu.make_async_remote_copy(
            src_ref=source, dst_ref=target,
            send_sem=send_sem.at[phase, peer], recv_sem=recv_sem.at[phase, origin],
            device_id=(peer, mine), device_id_type=mesh_ids,
        )

    at_end = []

    def spread(phase, b):
        few, many = few_ref.at[phase, b], many_ref.at[phase]
        size = few.shape[0]

        def copy_to(slot):
            return row_copy(
                phase, few.at[:, block(slot, own_chans), :], many.at[block(me, size)],
                slot * samples + b, me,
            )

        def each(act):
            for step in range(1, handlers):
                act(copy_to(lax.rem(my_slot + step, handlers)))

            @pl.when(my_sample != b)
            def _():
                act(copy_to(my_slot))

        each(lambda copy: copy.start())
        at_end.append(lambda: each(lambda copy: copy.wait_send()))

        @pl.when(my_sample == b)
        def _():
            many[block(me, size)] = few[:, block(my_slot, own_chans), :]

    def transform(phase, b, table_ref, scale):
        @pl.when(my_sample == b)
        def _():
            source, result_ref = many_ref.at[phase], many_ref.at[phase + 1]
            count = source.shape[0]
            size = count // ranks
            for step in range(1, ranks):
                origin = rank_at(step)
                here = source.at[block(origin, size)]
                row_copy(phase, here, here, origin, origin).wait_recv()
            for pair in range(own_chans):
                values = source[:, pair, :]
                crossed = jnp.where(even_lanes(values), next_lane(values), -prev_lane(values))
                here = slice(pair * lanes, (pair + 1) * lanes)
                for at, piece in enumerate((values, crossed)):
                    high, low = split_bf16(piece)
                    stack_ref[at * count:(at + 1) * count, here] = high
                    stack_ref[(2 + at) * count:(3 + at) * count, here] = low
                    stack_ref[(4 + at) * count:(5 + at) * count, here] = high
            result = jnp.dot(table_ref[...], stack_ref[...], preferred_element_type=jnp.float32)
            result = result * scale
            for pair in range(own_chans):
                result_ref[:, pair, :] = result[:, pair * lanes:(pair + 1) * lanes]
            few = few_ref.at[phase + 1, b]
            for step in range(1, ranks):
                peer = rank_at(step)
                row_copy(
                    phase + 1, result_ref.at[block(peer, size)],
                    few.at[:, block(my_slot, own_chans), :], peer, me,
                ).start()
            few[:, block(my_slot, own_chans), :] = result_ref[block(me, size)]

        def finish():
            @pl.when(my_sample == b)
            def _():
                size = many_ref.shape[1] // ranks
                for step in range(1, ranks):
                    peer = rank_at(step)
                    here = many_ref.at[phase + 1, block(peer, size)]
                    row_copy(phase + 1, here, here, peer, me).wait_send()

        at_end.append(finish)

    def collected(phase, b):
        few = few_ref.at[phase, b]

        def arrived(slot):
            here = few.at[:, block(slot, own_chans), :]
            origin = slot * samples + b
            row_copy(phase, here, here, origin, origin).wait_recv()

        for step in range(1, handlers):
            arrived(lax.rem(my_slot + step, handlers))

        @pl.when(my_sample != b)
        def _():
            arrived(my_slot)

        return few

    def mix_group(b, group, out_ref):
        outs = pl.ds(pl.multiple_of(group * chans, chans), chans)

        @pl.loop(0, kept_here)
        def _(k):
            plain = jnp.zeros((chans, lanes), jnp.float32)
            turned = jnp.zeros((chans, lanes), jnp.float32)
            for c in range(chans):
                w = weight_ref[k, c, outs, :]
                at = b * chans + c
                plain = plain + w * same_ref[k, at:at + 1, :]
                turned = turned + w * cross_ref[k, at:at + 1, :]
            out_ref[k] = plain + swap_pairs(turned)

    def group_copy(kind, b, step, source, target):
        return pltpu.make_async_remote_copy(
            src_ref=source, dst_ref=target,
            send_sem=ch_send.at[kind, b, step - 1], recv_sem=ch_recv.at[kind, b, step - 1],
            device_id=(me, group_at(step)), device_id_type=mesh_ids,
        )

    order = sorted(range(1, groups), key=lambda step: -min(step, groups - step))
    tile = 8

    def back_group(b, group, grad_ref, fresh):
        here = slice(b * chans, (b + 1) * chans)
        for k in range(kept_here):
            values = grad_ref[k]
            grads_ref[group, k, here, :] = values
            gswap_ref[group, k, here, :] = swap_pairs(values)

        @pl.loop(0, kept_here * (chans // tile))
        def _(at):
            k, first = at // (chans // tile), at % (chans // tile) * tile
            sums = [[None, None] for _ in range(tile)]
            for o in range(0, chans, tile):
                row = slice(b * chans + o, b * chans + o + tile)
                factors = (grads_ref[group, k, row, :], gswap_ref[group, k, row, :])
                outs = pl.ds(pl.multiple_of(group * chans + o, tile), tile)
                for c in range(tile):
                    w = weight_ref[k, first + c, outs, :]
                    for i, factor in enumerate(factors):
                        term = w * factor
                        sums[c][i] = term if sums[c][i] is None else sums[c][i] + term
            into = pl.ds(pl.multiple_of(first, tile), tile)
            for i, acc_ref in ((0, accp_ref), (1, accq_ref)):
                rows = [jnp.sum(sums[c][i], axis=0, keepdims=True) for c in range(tile)]
                total = jnp.concatenate(rows, axis=0)
                acc_ref[b, k, into, :] = total if fresh else acc_ref[b, k, into, :] + total

    def flow(b):
        for copy in load_field[b * rows_here:(b + 1) * rows_here]:
            copy.wait()
        few_ref[0, b] = analyze_cols(field_ref[b])
        if b == 0:
            pl.semaphore_wait(barrier, ranks - 1 + groups - 1)
        spread(0, b)
        yield
        transform(0, b, fwd_ref, scale_fwd)
        yield
        spectrum = collected(1, b)
        here = slice(b * chans, (b + 1) * chans)
        for k in range(kept_here):
            values = spectrum[k]
            even = even_lanes(values)
            same_ref[k, here, :] = jnp.where(even, values, prev_lane(values))
            cross_ref[k, here, :] = jnp.where(even, next_lane(values), -values)
        if b == 0:
            load_weight.wait()
        copies = []
        for step in order:
            part = part_ref.at[b, step - 1]
            mix_group(b, group_at(step), part)
            copy = group_copy(0, b, step, part, arrive_ref.at[b, step - 1])
            copy.start()
            copies.append(copy)
        mixed = few_ref.at[2, b]
        mix_group(b, mine, mixed)
        at_end.extend(copy.wait_send for copy in copies)
        yield
        for copy in copies:
            copy.wait_recv()
        for k in range(kept_here):
            total = mixed[k]
            for step in order:
                total = total + arrive_ref[b, step - 1, k]
            mixed[k] = total
        spread(2, b)
        yield
        transform(2, b, inv_ref, scale_inv)
        yield
        few = collected(3, b)
        for copy in load_cot[b * rows_here:(b + 1) * rows_here]:
            copy.wait()
        before = synth_cols(few[...]) + bias_rows
        slope = 0.5 * (1.0 + lax.erf(before * (1.0 / math.sqrt(2.0))))
        slope = slope + before * jnp.exp(-0.5 * before * before) * (1.0 / math.sqrt(2.0 * math.pi))
        few_ref[4, b] = analyze_cols(cot_ref[b].reshape(flat_rows, width) * slope)
        spread(4, b)
        yield
        transform(4, b, fwd_ref, scale_inv)
        yield
        own = collected(5, b)
        copies = []
        for step in order:
            copy = group_copy(1, b, step, own, gall_ref.at[b, mine])
            copy.start()
            copies.append(copy)
        at_end.extend(copy.wait_send for copy in copies)
        back_group(b, mine, own, True)
        yield
        for step in sorted(order, key=lambda step: min(step, groups - step)):
            copies[order.index(step)].wait_recv()
            source = lax.rem(mine + groups - step, groups)
            back_group(b, source, gall_ref.at[b, source], False)
        for k in range(kept_here):
            p, q = accp_ref[b, k], accq_ref[b, k]
            few_ref[6, b, k] = jnp.where(even_lanes(p), p + next_lane(p), prev_lane(q) - q)
        spread(6, b)
        yield
        transform(6, b, inv_ref, scale_fwd)
        yield
        few = collected(7, b)
        gfield_ref[b] = synth_cols(few[...]).reshape(rows_here, chans, width)
        for h in range(rows_here):
            copy = pltpu.make_async_copy(
                gfield_ref.at[b, h], gfield_hbm.at[b, :, h, :], field_sem.at[0, b, h]
            )
            copy.start()
            at_end.append(copy.wait)

    flows = [flow(b) for b in range(samples)]
    while flows:
        for one in list(flows):
            if next(one, flows) is flows:
                flows.remove(one)
    for act in at_end:
        act()


def weight_kernel(chans, samples, same_ref, cross_ref, grads_ref, gswap_ref, out_ref):
    tile, together = 8, 2
    count = out_ref.shape[1]
    first = pl.program_id(1) * count

    for c in range(0, count, together):
        same, cross = [
            [
                [ref[0, pl.ds(b * chans + first + c + i, 1), :] for b in range(samples)]
                for i in range(together)
            ]
            for ref in (same_ref, cross_ref)
        ]
        for group in range(grads_ref.shape[0]):
            for o in range(0, chans, tile):
                rows = [slice(b * chans + o, b * chans + o + tile) for b in range(samples)]
                plain = [grads_ref[group, 0, row, :] for row in rows]
                turned = [gswap_ref[group, 0, row, :] for row in rows]
                at = group * chans + o
                for i in range(together):
                    total = plain[0] * same[i][0] + turned[0] * cross[i][0]
                    for b in range(1, samples):
                        total = total + plain[b] * same[i][b] + turned[b] * cross[i][b]
                    out_ref[0, c + i, at:at + tile, :] = total


def kernel_fits(ranks, groups, field, weight, mode_rows, bias):
    pairs = field.shape[0] * field.shape[1]
    lanes = weight.shape[3]
    return (
        pairs % (8 * ranks) == 0 and ranks % field.shape[0] == 0 and lanes == 128 and field.shape[1] % 8 == 0
        and field.shape[1] * groups == weight.shape[2] and mode_rows.shape[0] % 32 == 0
        and field.shape[2] * ranks % 32 == 0 and mode_rows.shape[0] == field.shape[2] * ranks
        and field.shape[3] % 128 == 0 and bias.shape[0] % 128 == 0
    )


def kernel_body(field, cotangent, weight, bias, mode_rows, mode_cols):
    samples, chans, rows_here, width = field.shape
    ranks, groups = lax.axis_size("rows"), lax.axis_size("ch")
    kept, lanes = mode_rows.shape[0], weight.shape[3]
    grid_rows = rows_here * ranks
    kept_here = kept // ranks
    pairs = samples * chans
    own_chans = pairs // ranks
    f32, bf16, i32 = jnp.float32, jnp.bfloat16, jnp.int32
    sizes = (samples, chans, rows_here, width, kept, ranks, groups, lanes)
    vmem = pl.BlockSpec(memory_space=pltpu.VMEM)
    hbm = pl.BlockSpec(memory_space=pl.ANY)
    modes = (kept_here, pairs, lanes)
    slab = (kept_here, chans, lanes)
    by_row = (samples, rows_here, chans, width)
    dma = pltpu.SemaphoreType.DMA
    gfield, same, cross, grads, gswap = pl.pallas_call(
        functools.partial(layer_kernel, sizes),
        out_shape=(
            jax.ShapeDtypeStruct(field.shape, f32),
            jax.ShapeDtypeStruct(modes, f32),
            jax.ShapeDtypeStruct(modes, f32),
            jax.ShapeDtypeStruct((groups,) + modes, f32),
            jax.ShapeDtypeStruct((groups,) + modes, f32),
        ),
        in_specs=[hbm] * 6,
        out_specs=(hbm,) + (vmem,) * 4,
        scratch_shapes=[
            pltpu.VMEM(weight.shape, f32),
            pltpu.VMEM(by_row, f32),
            pltpu.VMEM(by_row, f32),
            pltpu.VMEM(by_row, f32),
            pltpu.VMEM((1, bias.shape[0]), f32),
            pltpu.VMEM((1, lanes // 2), i32),
            pltpu.VMEM((1, kept), i32),
            pltpu.VMEM((width, lanes), bf16),
            pltpu.VMEM((width, lanes), bf16),
            pltpu.VMEM((kept, 6 * grid_rows), bf16),
            pltpu.VMEM((grid_rows, 6 * kept), bf16),
            pltpu.VMEM((6 * kept, own_chans * lanes), bf16),
            pltpu.VMEM((8, samples) + slab, f32),
            pltpu.VMEM((8, grid_rows, own_chans, lanes), f32),
            pltpu.VMEM((samples, groups - 1) + slab, f32),
            pltpu.VMEM((samples, groups - 1) + slab, f32),
            pltpu.VMEM((samples, groups) + slab, f32),
            pltpu.VMEM((samples,) + slab, f32),
            pltpu.VMEM((samples,) + slab, f32),
            dma((4,)),
            dma((2, samples, rows_here)),
            dma((8, ranks)),
            dma((8, ranks)),
            dma((2, samples, groups - 1)),
            dma((2, samples, groups - 1)),
        ],
        compiler_params=pltpu.CompilerParams(
            collective_id=0, has_side_effects=True, vmem_limit_bytes=52 * 1024 * 1024
        ),
    )(
        field, cotangent, weight,
        bias.reshape(1, bias.shape[0]),
        mode_cols.reshape(1, lanes // 2),
        mode_rows.reshape(1, kept),
    )
    count = 8
    one = pl.BlockSpec((1, pairs, lanes), lambda k, c: (k, 0, 0))
    every = pl.BlockSpec((groups, 1, pairs, lanes), lambda k, c: (0, k, 0, 0))
    gweight = pl.pallas_call(
        functools.partial(weight_kernel, chans, samples),
        out_shape=jax.ShapeDtypeStruct(weight.shape, f32),
        grid=(kept_here, chans // count),
        in_specs=[one, one, every, every],
        out_specs=pl.BlockSpec((1, count) + weight.shape[2:], lambda k, c: (k, c, 0, 0)),
        compiler_params=pltpu.CompilerParams(vmem_limit_bytes=32 * 1024 * 1024),
    )(same, cross, grads, gswap)
    return gfield, gweight


def any_body(field, cotangent, weight, bias, mode_rows, mode_cols):
    ranks, groups = lax.axis_size("rows"), lax.axis_size("ch")
    chosen = kernel_body if kernel_fits(ranks, groups, field, weight, mode_rows, bias) else body
    return chosen(field, cotangent, weight, bias, mode_rows, mode_cols)


def solution(mesh):
    return jax.shard_map(
        any_body,
        mesh=mesh,
        in_specs=(
            P(None, "ch", "rows", None),
            P(None, "ch", "rows", None),
            P("rows", "ch", None, None),
            P(),
            P(),
            P(),
        ),
        out_specs=(P(None, "ch", "rows", None), P("rows", "ch", None, None)),
        check_vma=False,
    )
```

```python
import functools
import math

import jax
import jax.numpy as jnp
from jax import lax
from jax.experimental import pallas as pl
from jax.experimental.pallas import tpu as pltpu
from jax.sharding import PartitionSpec as P

precise_mode = lax.Precision.HIGHEST


def angle_table(modes, positions, length):
    phase = modes[:, None] * positions[None, :] % length
    return phase.astype(jnp.float32) * (2.0 * math.pi / length)


def column_table(mode_cols, length):
    angles = angle_table(mode_cols, jnp.arange(length, dtype=jnp.int32), length)
    stacked = jnp.stack([jnp.cos(angles), -jnp.sin(angles)], axis=1)
    return stacked.reshape(2 * mode_cols.shape[0], length)


def row_table(modes, positions, length):
    angles = angle_table(modes, positions, length)
    return jnp.concatenate([jnp.cos(angles), jnp.sin(angles)], axis=0)


def split_parts(values):
    shaped = values.reshape(values.shape[:-1] + (values.shape[-1] // 2, 2))
    return (shaped[..., 0], shaped[..., 1])


def join_parts(real, imag):
    return jnp.stack([real, imag], axis=-1).reshape(real.shape[:-1] + (2 * real.shape[-1],))


def analyze_rows(columns, table):
    count = table.shape[0] // 2
    shaped = columns.reshape(columns.shape[:-1] + (columns.shape[-1] // 2, 2))
    both = jnp.einsum("kh,bchmp->kbcmp", table, shaped, precision=precise_mode)
    cosine, sine = (both[:count], both[count:])
    return join_parts(cosine[..., 0] + sine[..., 1], cosine[..., 1] - sine[..., 0])


def synth_rows(modes, table):
    count = modes.shape[0]
    shaped = modes.reshape(modes.shape[:-1] + (modes.shape[-1] // 2, 2))
    cosine = jnp.einsum("kh,kbomp->bohmp", table[:count], shaped, precision=precise_mode)
    sine = jnp.einsum("kh,kbomp->bohmp", table[count:], shaped, precision=precise_mode)
    return join_parts(cosine[..., 0] - sine[..., 1], cosine[..., 1] + sine[..., 0])


def mix_modes(spectrum, weight):
    spec_re, spec_im = split_parts(spectrum)
    wgt_re, wgt_im = split_parts(weight)

    def contract(left, right):
        return jnp.einsum("kbcm,kcom->kbom", left, right, precision=precise_mode)

    real = contract(spec_re, wgt_re) - contract(spec_im, wgt_im)
    imag = contract(spec_re, wgt_im) + contract(spec_im, wgt_re)
    return join_parts(real, imag)


def mix_grads(spectrum, weight, grad_mixed):
    spec_re, spec_im = split_parts(spectrum)
    wgt_re, wgt_im = split_parts(weight)
    grad_re, grad_im = split_parts(grad_mixed)

    def outer(left, right):
        return jnp.einsum("kbom,kbcm->kcom", left, right, precision=precise_mode)

    def inner(left, right):
        return jnp.einsum("kcom,kbom->kbcm", left, right, precision=precise_mode)

    weight_re = outer(grad_re, spec_re) + outer(grad_im, spec_im)
    weight_im = outer(grad_im, spec_re) - outer(grad_re, spec_im)
    input_re = inner(wgt_re, grad_re) + inner(wgt_im, grad_im)
    input_im = inner(wgt_re, grad_im) - inner(wgt_im, grad_re)
    return (join_parts(weight_re, weight_im), join_parts(input_re, input_im))


def gelu_slope(values):
    cumulative = 0.5 * (1.0 + jax.scipy.special.erf(values / math.sqrt(2.0)))
    density = jnp.exp(-0.5 * values * values) / math.sqrt(2.0 * math.pi)
    return cumulative + values * density


def body(field, cotangent, weight, bias, mode_rows, mode_cols):
    rows_here = field.shape[2]
    row_count = lax.axis_size("rows")
    grid_rows = rows_here * row_count
    grid_cols = field.shape[3]
    all_rows = jnp.arange(grid_rows, dtype=jnp.int32)
    table_w = column_table(mode_cols, grid_cols)
    scale_fwd = 1.0 / math.sqrt(grid_rows * grid_cols)
    scale_inv = 1.0 / math.sqrt(mode_rows.shape[0] * mode_cols.shape[0])

    def analyze(values):
        columns = jnp.dot(
            values, table_w.T, precision=precise_mode, preferred_element_type=jnp.float32
        )
        spread = lax.all_to_all(columns, "rows", split_axis=3, concat_axis=2, tiled=True)
        pieces = analyze_rows(spread, row_table(mode_rows, all_rows, grid_rows))
        return lax.all_to_all(pieces, "rows", split_axis=0, concat_axis=3, tiled=True)

    def synthesize(modes):
        spread = lax.all_to_all(modes, "rows", split_axis=3, concat_axis=0, tiled=True)
        pieces = synth_rows(spread, row_table(mode_rows, all_rows, grid_rows))
        gathered = lax.all_to_all(pieces, "rows", split_axis=2, concat_axis=3, tiled=True)
        return jnp.dot(
            gathered, table_w, precision=precise_mode, preferred_element_type=jnp.float32
        )

    spectrum = analyze(field) * scale_fwd
    mixed = lax.psum_scatter(mix_modes(spectrum, weight), "ch", scatter_dimension=2, tiled=True)
    outputs_here = mixed.shape[2]
    bias_here = lax.dynamic_slice_in_dim(bias, lax.axis_index("ch") * outputs_here, outputs_here)
    before = synthesize(mixed) * scale_inv + bias_here[None, :, None, None]
    grad_before = cotangent * gelu_slope(before)
    grad_mixed = analyze(grad_before) * scale_inv
    grad_whole = lax.all_gather(grad_mixed, "ch", axis=2, tiled=True)
    grad_weight, grad_spectrum = mix_grads(spectrum, weight, grad_whole)
    grad_field = synthesize(grad_spectrum) * scale_fwd
    return (grad_field, grad_weight)


def split_bf16(values):
    high = values.astype(jnp.bfloat16)
    low = (values - high.astype(jnp.float32)).astype(jnp.bfloat16)
    return high, low


def turn_cosine(step, length):
    step = lax.rem(step, jnp.int32(length)) if length & (length - 1) else step & (length - 1)
    folded = jnp.abs(step - length // 2) - length // 4
    angle = folded.astype(jnp.float32) * (2.0 * math.pi / length)
    square = angle * angle
    total = jnp.float32(-2.5052108e-08)
    for factor in (2.7557319e-06, -1.9841270e-04, 8.3333333e-03, -1.6666667e-01):
        total = total * square + factor
    return angle + angle * square * total


def next_lane(values):
    return pltpu.roll(values, values.shape[-1] - 1, values.ndim - 1)


def prev_lane(values):
    return pltpu.roll(values, 1, values.ndim - 1)


def even_lanes(values):
    return lax.broadcasted_iota(jnp.int32, values.shape, values.ndim - 1) % 2 == 0


def swap_pairs(values):
    return jnp.where(even_lanes(values), next_lane(values), prev_lane(values))


def swap_rows(values, distance):
    row = lax.broadcasted_iota(jnp.int32, values.shape, 0)
    ahead = pltpu.roll(values, values.shape[0] - distance, 0)
    behind = pltpu.roll(values, distance, 0)
    return jnp.where(row // distance % 2 == 0, ahead, behind)


def row_sums(tiles):
    count = len(tiles)
    row = lax.broadcasted_iota(jnp.int32, tiles[0].shape, 0)
    while len(tiles) > 1:
        half = len(tiles) // 2
        first = row // half % 2 == 0
        merged = []
        for one, two in zip(tiles[:half], tiles[half:]):
            stay, move = jnp.where(first, one, two), jnp.where(first, two, one)
            moved = pltpu.roll(move, half, 0) if 2 * half == count else swap_rows(move, half)
            merged.append(stay + moved)
        tiles = merged
    return tiles[0]


def layer_kernel(
    sizes, field_hbm, cot_hbm, weight_hbm, bias_hbm, colmode_hbm, rowmode_hbm,
    gfield_ref, same_ref, cross_ref, grads_ref, gswap_ref,
    weight_ref, field_ref, cot_ref, bias_ref, colmode_ref, rowmode_ref,
    analysis_ref, synthesis_ref, fwd_ref, inv_ref, stack_ref,
    few_ref, many_ref, part_ref, arrive_ref, gall_ref, acc_ref,
    local_sem, field_sem, send_sem, recv_sem, ch_send, ch_recv,
):
    samples, chans, rows_here, width, kept, ranks, groups, lanes = sizes
    grid_rows = rows_here * ranks
    kept_here = kept // ranks
    handlers = ranks // samples
    own_chans = chans // handlers
    flat_rows = chans * rows_here
    scale_fwd = 1.0 / math.sqrt(grid_rows * width)
    scale_inv = 1.0 / math.sqrt(kept * (lanes // 2))
    me, mine = lax.axis_index("rows"), lax.axis_index("ch")
    my_sample, my_slot = lax.rem(me, samples), me // samples
    mesh_ids = pl.DeviceIdType.MESH

    def rank_at(step):
        return lax.rem(me + step, ranks)

    def group_at(step):
        return lax.rem(mine + step, groups)

    barrier = pltpu.get_barrier_semaphore()
    for step in range(1, ranks):
        pl.semaphore_signal(barrier, inc=1, device_id=(rank_at(step), mine), device_id_type=mesh_ids)
    for step in range(1, groups):
        pl.semaphore_signal(barrier, inc=1, device_id=(me, group_at(step)), device_id_type=mesh_ids)

    loads = []
    for at, (source, target) in enumerate((
        (colmode_hbm, colmode_ref), (rowmode_hbm, rowmode_ref), (bias_hbm, bias_ref),
    )):
        load = pltpu.make_async_copy(source, target, local_sem.at[at])
        load.start()
        loads.append(load)

    def row_copies(source, target, kind):
        found = []
        for b in range(samples):
            for h in range(rows_here):
                copy = pltpu.make_async_copy(
                    source.at[b, :, h, :], target.at[b, h], field_sem.at[kind, b, h]
                )
                copy.start()
                found.append(copy)
        return found

    load_field = row_copies(field_hbm, field_ref, 0)
    load_weight = pltpu.make_async_copy(weight_hbm, weight_ref, local_sem.at[3])
    load_weight.start()
    load_cot = row_copies(cot_hbm, cot_ref, 1)
    for load in loads:
        load.wait()

    def as_column(values):
        count = values.shape[1]
        row = lax.broadcasted_iota(jnp.int32, (count, count), 0)
        lane = lax.broadcasted_iota(jnp.int32, (count, count), 1)
        kept_values = jnp.where(row == lane, values.astype(jnp.float32), 0.0)
        return jnp.sum(kept_values, axis=1, keepdims=True)

    def pick(column, index):
        row = lax.broadcasted_iota(jnp.int32, (column.shape[0], index.shape[1]), 0)
        return jnp.sum(jnp.where(row == index, column, 0.0), axis=0, keepdims=True).astype(jnp.int32)

    col_column = as_column(colmode_ref[...])
    col_lanes = pick(col_column, lax.broadcasted_iota(jnp.int32, (1, lanes), 1) // 2)
    row_column = as_column(rowmode_ref[...])
    row_lanes = pick(row_column, lax.broadcasted_iota(jnp.int32, (1, 6 * kept), 1) % kept)
    row_column = row_column.astype(jnp.int32)
    chunk = 128

    @pl.loop(0, width // chunk)
    def _(at):
        shape = (chunk, lanes)
        column = lax.broadcasted_iota(jnp.int32, shape, 0) + at * chunk
        quarter = lax.broadcasted_iota(jnp.int32, shape, 1) % 2 * (width // 4)
        high, low = split_bf16(turn_cosine(col_lanes * column + quarter, width))
        here = pl.ds(pl.multiple_of(at * chunk, chunk), chunk)
        analysis_ref[here, :lanes] = high
        analysis_ref[here, lanes:] = low

    def fill_synthesis():
        modes = as_column(col_lanes).astype(jnp.int32)

        @pl.loop(0, width // chunk)
        def _(at):
            shape = (lanes, chunk)
            column = lax.broadcasted_iota(jnp.int32, shape, 1) + at * chunk
            quarter = lax.broadcasted_iota(jnp.int32, shape, 0) % 2 * (width // 4)
            high, low = split_bf16(turn_cosine(modes * column + quarter, width))
            here = pl.ds(pl.multiple_of(at * chunk, chunk), chunk)
            synthesis_ref[:lanes, here] = high
            synthesis_ref[lanes:2 * lanes, here] = low
            synthesis_ref[2 * lanes:, here] = high

    def packed_table(step, length):
        table = turn_cosine(step, length)
        high, low = split_bf16(table)
        lane = lax.broadcasted_iota(jnp.int32, table.shape, 1)
        edge = table.shape[1] // 3 * 2
        chosen = jnp.where(lane < edge, high.astype(jnp.float32), low.astype(jnp.float32))
        return chosen.astype(jnp.bfloat16)

    spot = lax.broadcasted_iota(jnp.int32, (kept, 6 * grid_rows), 1)
    turn = spot // grid_rows % 2 * (3 * grid_rows // 4)
    fwd_ref[...] = packed_table(row_column * (spot % grid_rows) + turn, grid_rows)
    spot = lax.broadcasted_iota(jnp.int32, (grid_rows, 6 * kept), 1)
    turn = spot // kept % 2 * (grid_rows // 4)
    row = lax.broadcasted_iota(jnp.int32, (grid_rows, 6 * kept), 0)
    inv_ref[...] = packed_table(row_lanes * row + turn, grid_rows)
    whole = bias_ref.shape[1]
    out_chan = mine * chans + lax.broadcasted_iota(jnp.int32, (flat_rows, whole), 0) % chans
    picked = lax.broadcasted_iota(jnp.int32, (flat_rows, whole), 1) == out_chan
    bias_rows = jnp.sum(jnp.where(picked, bias_ref[...], 0.0), axis=1, keepdims=True)

    def analyze_cols(values):
        high, low = split_bf16(values.reshape(flat_rows, width))
        both = jnp.concatenate([high, low], axis=0)
        result = jnp.dot(both, analysis_ref[...], preferred_element_type=jnp.float32)
        top = result[:flat_rows, :lanes] + (
            result[:flat_rows, lanes:] + result[flat_rows:, :lanes]
        )
        return top.reshape(rows_here, chans, lanes)

    def synth_cols(values):
        high, low = split_bf16(values.reshape(flat_rows, lanes))
        packed = jnp.concatenate([high, high, low], axis=1)
        return jnp.dot(packed, synthesis_ref[...], preferred_element_type=jnp.float32)

    def block(rank, size):
        return pl.ds(pl.multiple_of(rank * size, size), size)

    def row_copy(phase, source, target, peer, origin):
        return pltpu.make_async_remote_copy(
            src_ref=source, dst_ref=target,
            send_sem=send_sem.at[phase, peer], recv_sem=recv_sem.at[phase, origin],
            device_id=(peer, mine), device_id_type=mesh_ids,
        )

    at_end = []

    def spread(phase, b):
        few, many = few_ref.at[phase, b], many_ref.at[phase]
        size = few.shape[0]

        def copy_to(slot):
            return row_copy(
                phase, few.at[:, block(slot, own_chans), :], many.at[block(me, size)],
                slot * samples + b, me,
            )

        def each(act):
            for step in range(1, handlers):
                act(copy_to(lax.rem(my_slot + step, handlers)))

            @pl.when(my_sample != b)
            def _():
                act(copy_to(my_slot))

        each(lambda copy: copy.start())
        at_end.append(lambda: each(lambda copy: copy.wait_send()))

        @pl.when(my_sample == b)
        def _():
            many[block(me, size)] = few[:, block(my_slot, own_chans), :]

    def transform(phase, b, table_ref, scale):
        @pl.when(my_sample == b)
        def _():
            source, result_ref = many_ref.at[phase], many_ref.at[phase + 1]
            count = source.shape[0]
            size = count // ranks
            for step in range(1, ranks):
                origin = rank_at(step)
                here = source.at[block(origin, size)]
                row_copy(phase, here, here, origin, origin).wait_recv()
            for pair in range(own_chans):
                values = source[:, pair, :]
                crossed = jnp.where(even_lanes(values), next_lane(values), -prev_lane(values))
                here = slice(pair * lanes, (pair + 1) * lanes)
                for at, piece in enumerate((values, crossed)):
                    high, low = split_bf16(piece)
                    stack_ref[at * count:(at + 1) * count, here] = high
                    stack_ref[(2 + at) * count:(3 + at) * count, here] = low
                    stack_ref[(4 + at) * count:(5 + at) * count, here] = high
            result = jnp.dot(table_ref[...], stack_ref[...], preferred_element_type=jnp.float32)
            result = result * scale
            for pair in range(own_chans):
                result_ref[:, pair, :] = result[:, pair * lanes:(pair + 1) * lanes]
            few = few_ref.at[phase + 1, b]
            for step in range(1, ranks):
                peer = rank_at(step)
                row_copy(
                    phase + 1, result_ref.at[block(peer, size)],
                    few.at[:, block(my_slot, own_chans), :], peer, me,
                ).start()
            few[:, block(my_slot, own_chans), :] = result_ref[block(me, size)]

        def finish():
            @pl.when(my_sample == b)
            def _():
                size = many_ref.shape[1] // ranks
                for step in range(1, ranks):
                    peer = rank_at(step)
                    here = many_ref.at[phase + 1, block(peer, size)]
                    row_copy(phase + 1, here, here, peer, me).wait_send()

        at_end.append(finish)

    def collected(phase, b):
        few = few_ref.at[phase, b]

        def arrived(slot):
            here = few.at[:, block(slot, own_chans), :]
            origin = slot * samples + b
            row_copy(phase, here, here, origin, origin).wait_recv()

        for step in range(1, handlers):
            arrived(lax.rem(my_slot + step, handlers))

        @pl.when(my_sample != b)
        def _():
            arrived(my_slot)

        return few

    def mix_group(b, group, out_ref):
        outs = pl.ds(pl.multiple_of(group * chans, chans), chans)

        @pl.loop(0, kept_here)
        def _(k):
            plain = jnp.zeros((chans, lanes), jnp.float32)
            turned = jnp.zeros((chans, lanes), jnp.float32)
            for c in range(chans):
                w = weight_ref[k, c, outs, :]
                at = b * chans + c
                plain = plain + w * same_ref[k, at:at + 1, :]
                turned = turned + w * cross_ref[k, at:at + 1, :]
            out_ref[k] = plain + swap_pairs(turned)

    def group_copy(kind, b, step, source, target):
        return pltpu.make_async_remote_copy(
            src_ref=source, dst_ref=target,
            send_sem=ch_send.at[kind, b, step - 1], recv_sem=ch_recv.at[kind, b, step - 1],
            device_id=(me, group_at(step)), device_id_type=mesh_ids,
        )

    order = sorted(range(1, groups), key=lambda step: -min(step, groups - step))
    tile = 8

    def back_group(b, group, grad_ref, fresh, last):
        here = slice(b * chans, (b + 1) * chans)
        for k in range(kept_here):
            values = grad_ref[k]
            grads_ref[group, k, here, :] = values
            gswap_ref[group, k, here, :] = swap_pairs(values)

        @pl.loop(0, kept_here * (chans // tile))
        def _(at):
            k, first = at // (chans // tile), at % (chans // tile) * tile
            sums = [[None, None] for _ in range(tile)]
            for o in range(0, chans, tile):
                row = slice(b * chans + o, b * chans + o + tile)
                factors = (grads_ref[group, k, row, :], gswap_ref[group, k, row, :])
                outs = pl.ds(pl.multiple_of(group * chans + o, tile), tile)
                for c in range(tile):
                    w = weight_ref[k, first + c, outs, :]
                    for i, factor in enumerate(factors):
                        term = w * factor
                        sums[c][i] = term if sums[c][i] is None else sums[c][i] + term
            for i in range(2):
                for c in range(tile):
                    if not fresh:
                        sums[c][i] = sums[c][i] + acc_ref[b, at, i, c]
                    if not last:
                        acc_ref[b, at, i, c] = sums[c][i]
            if last:
                p, q = (row_sums([pair[i] for pair in sums]) for i in range(2))
                into = pl.ds(pl.multiple_of(first, tile), tile)
                few_ref[6, b, k, into, :] = jnp.where(
                    even_lanes(p), p + next_lane(p), prev_lane(q) - q
                )

    def flow(b):
        for copy in load_field[b * rows_here:(b + 1) * rows_here]:
            copy.wait()
        few_ref[0, b] = analyze_cols(field_ref[b])
        if b == 0:
            pl.semaphore_wait(barrier, ranks - 1 + groups - 1)
        spread(0, b)
        if b == samples - 1:
            fill_synthesis()
        yield
        transform(0, b, fwd_ref, scale_fwd)
        yield
        spectrum = collected(1, b)
        here = slice(b * chans, (b + 1) * chans)
        for k in range(kept_here):
            values = spectrum[k]
            even = even_lanes(values)
            same_ref[k, here, :] = jnp.where(even, values, prev_lane(values))
            cross_ref[k, here, :] = jnp.where(even, next_lane(values), -values)
        if b == 0:
            load_weight.wait()
        copies = []
        for step in order:
            part = part_ref.at[b, step - 1]
            mix_group(b, group_at(step), part)
            copy = group_copy(0, b, step, part, arrive_ref.at[b, step - 1])
            copy.start()
            copies.append(copy)
        mixed = few_ref.at[2, b]
        mix_group(b, mine, mixed)
        at_end.extend(copy.wait_send for copy in copies)
        yield
        for copy in copies:
            copy.wait_recv()
        for k in range(kept_here):
            total = mixed[k]
            for step in order:
                total = total + arrive_ref[b, step - 1, k]
            mixed[k] = total
        spread(2, b)
        yield
        transform(2, b, inv_ref, scale_inv)
        yield
        few = collected(3, b)
        for copy in load_cot[b * rows_here:(b + 1) * rows_here]:
            copy.wait()
        before = synth_cols(few[...]) + bias_rows
        slope = 0.5 * (1.0 + lax.erf(before * (1.0 / math.sqrt(2.0))))
        slope = slope + before * jnp.exp(-0.5 * before * before) * (1.0 / math.sqrt(2.0 * math.pi))
        few_ref[4, b] = analyze_cols(cot_ref[b].reshape(flat_rows, width) * slope)
        spread(4, b)
        yield
        transform(4, b, fwd_ref, scale_inv)
        yield
        own = collected(5, b)
        copies = []
        for step in order:
            copy = group_copy(1, b, step, own, gall_ref.at[b, mine])
            copy.start()
            copies.append(copy)
        at_end.extend(copy.wait_send for copy in copies)
        back_group(b, mine, own, True, groups == 1)
        yield
        near = sorted(order, key=lambda step: min(step, groups - step))
        for step in near:
            copies[order.index(step)].wait_recv()
            source = lax.rem(mine + groups - step, groups)
            back_group(b, source, gall_ref.at[b, source], False, step == near[-1])
        spread(6, b)
        yield
        transform(6, b, inv_ref, scale_fwd)
        yield
        few = collected(7, b)
        gfield_ref[b] = synth_cols(few[...]).reshape(rows_here, chans, width)

    flows = [flow(b) for b in range(samples)]
    stages = 11
    lag = [[0, 1, 2], [3, 4], [5], [6], [7], [8, 9], [10]]
    follow = [[0, 1, 2], [3], [4], [5], [6, 7], [8], [9, 10]]
    assert sum(map(len, lag)) == sum(map(len, follow)) == stages
    turns = [0, 1, 0, 1, 0, 1]
    for ahead, behind in zip(lag[1:], follow[1:]):
        turns += [0] * len(ahead) + [1] * len(behind)
    for turn in turns:
        for one in flows[:1] if turn == 0 else flows[1:]:
            next(one, None)
    for act in at_end:
        act()


def output_kernel(
    same_ref, cross_ref, grads_ref, gswap_ref, rows_hbm, gfield_hbm, gweight_hbm,
    gweight_ref, field_sem, weight_sem,
):
    samples, rows_here, chans = rows_hbm.shape[:3]
    groups, kept_here = grads_ref.shape[:2]
    tile, together, count = 8, 2, 8
    copies = []
    for b in range(samples):
        for h in range(rows_here):
            copy = pltpu.make_async_copy(
                rows_hbm.at[b, h], gfield_hbm.at[b, :, h, :], field_sem.at[b, h]
            )
            copy.start()
            copies.append(copy)

    def weight_copy(at):
        k, first = at // (chans // count), at % (chans // count) * count
        here = pl.ds(first, count)
        return pltpu.make_async_copy(
            gweight_ref.at[k, here], gweight_hbm.at[k, here], weight_sem.at[at]
        )

    @pl.loop(0, kept_here * (chans // count))
    def _(at):
        k, first = at // (chans // count), at % (chans // count) * count
        for c in range(0, count, together):
            same, cross = [
                [
                    [ref[k, pl.ds(b * chans + first + c + i, 1), :] for b in range(samples)]
                    for i in range(together)
                ]
                for ref in (same_ref, cross_ref)
            ]
            for group in range(groups):
                for o in range(0, chans, tile):
                    rows = [slice(b * chans + o, b * chans + o + tile) for b in range(samples)]
                    plain = [grads_ref[group, k, row, :] for row in rows]
                    turned = [gswap_ref[group, k, row, :] for row in rows]
                    out = group * chans + o
                    for i in range(together):
                        total = plain[0] * same[i][0] + turned[0] * cross[i][0]
                        for b in range(1, samples):
                            total = total + plain[b] * same[i][b] + turned[b] * cross[i][b]
                        gweight_ref[k, first + c + i, out:out + tile, :] = total
        weight_copy(at).start()

    @pl.loop(0, kept_here * (chans // count))
    def _(at):
        weight_copy(at).wait()

    for copy in copies:
        copy.wait()


def kernel_fits(ranks, groups, field, weight, mode_rows, bias):
    pairs = field.shape[0] * field.shape[1]
    lanes = weight.shape[3]
    return (
        pairs % (8 * ranks) == 0 and ranks % field.shape[0] == 0 and lanes == 128 and field.shape[1] % 8 == 0
        and field.shape[1] * groups == weight.shape[2] and mode_rows.shape[0] % 32 == 0
        and field.shape[2] * ranks % 32 == 0 and mode_rows.shape[0] == field.shape[2] * ranks
        and field.shape[3] % 128 == 0 and bias.shape[0] % 128 == 0
    )


def kernel_body(field, cotangent, weight, bias, mode_rows, mode_cols):
    samples, chans, rows_here, width = field.shape
    ranks, groups = lax.axis_size("rows"), lax.axis_size("ch")
    kept, lanes = mode_rows.shape[0], weight.shape[3]
    grid_rows = rows_here * ranks
    kept_here = kept // ranks
    pairs = samples * chans
    own_chans = pairs // ranks
    f32, bf16, i32 = jnp.float32, jnp.bfloat16, jnp.int32
    sizes = (samples, chans, rows_here, width, kept, ranks, groups, lanes)
    vmem = pl.BlockSpec(memory_space=pltpu.VMEM)
    hbm = pl.BlockSpec(memory_space=pltpu.HBM)
    modes = (kept_here, pairs, lanes)
    slab = (kept_here, chans, lanes)
    by_row = (samples, rows_here, chans, width)
    dma = pltpu.SemaphoreType.DMA
    rows, same, cross, grads, gswap = pl.pallas_call(
        functools.partial(layer_kernel, sizes),
        out_shape=(
            jax.ShapeDtypeStruct(by_row, f32),
            jax.ShapeDtypeStruct(modes, f32),
            jax.ShapeDtypeStruct(modes, f32),
            jax.ShapeDtypeStruct((groups,) + modes, f32),
            jax.ShapeDtypeStruct((groups,) + modes, f32),
        ),
        in_specs=[hbm] * 6,
        out_specs=(vmem,) * 5,
        scratch_shapes=[
            pltpu.VMEM(weight.shape, f32),
            pltpu.VMEM(by_row, f32),
            pltpu.VMEM(by_row, f32),
            pltpu.VMEM((1, bias.shape[0]), f32),
            pltpu.VMEM((1, lanes // 2), i32),
            pltpu.VMEM((1, kept), i32),
            pltpu.VMEM((width, 2 * lanes), bf16),
            pltpu.VMEM((3 * lanes, width), bf16),
            pltpu.VMEM((kept, 6 * grid_rows), bf16),
            pltpu.VMEM((grid_rows, 6 * kept), bf16),
            pltpu.VMEM((6 * kept, own_chans * lanes), bf16),
            pltpu.VMEM((8, samples) + slab, f32),
            pltpu.VMEM((8, grid_rows, own_chans, lanes), f32),
            pltpu.VMEM((samples, groups - 1) + slab, f32),
            pltpu.VMEM((samples, groups - 1) + slab, f32),
            pltpu.VMEM((samples, groups) + slab, f32),
            pltpu.VMEM((samples, kept_here * chans // 8, 2, 8, 8, lanes), f32),
            dma((4,)),
            dma((2, samples, rows_here)),
            dma((8, ranks)),
            dma((8, ranks)),
            dma((2, samples, groups - 1)),
            dma((2, samples, groups - 1)),
        ],
        compiler_params=pltpu.CompilerParams(
            collective_id=0, has_side_effects=True, vmem_limit_bytes=52 * 1024 * 1024
        ),
    )(
        field, cotangent, weight,
        bias.reshape(1, bias.shape[0]),
        mode_cols.reshape(1, lanes // 2),
        mode_rows.reshape(1, kept),
    )
    gfield, gweight = pl.pallas_call(
        output_kernel,
        out_shape=(
            jax.ShapeDtypeStruct(field.shape, f32), jax.ShapeDtypeStruct(weight.shape, f32),
        ),
        in_specs=[vmem] * 4 + [pl.BlockSpec(memory_space=pl.ANY)],
        out_specs=(hbm, hbm),
        scratch_shapes=[
            pltpu.VMEM(weight.shape, f32),
            dma((samples, rows_here)),
            dma((kept_here * chans // 8,)),
        ],
        compiler_params=pltpu.CompilerParams(vmem_limit_bytes=32 * 1024 * 1024),
    )(same, cross, grads, gswap, rows)
    return gfield, gweight


def any_body(field, cotangent, weight, bias, mode_rows, mode_cols):
    ranks, groups = lax.axis_size("rows"), lax.axis_size("ch")
    chosen = kernel_body if kernel_fits(ranks, groups, field, weight, mode_rows, bias) else body
    return chosen(field, cotangent, weight, bias, mode_rows, mode_cols)


def solution(mesh):
    return jax.shard_map(
        any_body,
        mesh=mesh,
        in_specs=(
            P(None, "ch", "rows", None),
            P(None, "ch", "rows", None),
            P("rows", "ch", None, None),
            P(),
            P(),
            P(),
        ),
        out_specs=(P(None, "ch", "rows", None), P("rows", "ch", None, None)),
        check_vma=False,
    )
```

```python
import functools
import math

import jax
import jax.numpy as jnp
from jax import lax
from jax.experimental import pallas as pl
from jax.experimental.pallas import tpu as pltpu
from jax.sharding import PartitionSpec as P

precise_mode = lax.Precision.HIGHEST


def angle_table(modes, positions, length):
    phase = modes[:, None] * positions[None, :] % length
    return phase.astype(jnp.float32) * (2.0 * math.pi / length)


def column_table(mode_cols, length):
    angles = angle_table(mode_cols, jnp.arange(length, dtype=jnp.int32), length)
    stacked = jnp.stack([jnp.cos(angles), -jnp.sin(angles)], axis=1)
    return stacked.reshape(2 * mode_cols.shape[0], length)


def row_table(modes, positions, length):
    angles = angle_table(modes, positions, length)
    return jnp.concatenate([jnp.cos(angles), jnp.sin(angles)], axis=0)


def split_parts(values):
    shaped = values.reshape(values.shape[:-1] + (values.shape[-1] // 2, 2))
    return (shaped[..., 0], shaped[..., 1])


def join_parts(real, imag):
    return jnp.stack([real, imag], axis=-1).reshape(real.shape[:-1] + (2 * real.shape[-1],))


def analyze_rows(columns, table):
    count = table.shape[0] // 2
    shaped = columns.reshape(columns.shape[:-1] + (columns.shape[-1] // 2, 2))
    both = jnp.einsum("kh,bchmp->kbcmp", table, shaped, precision=precise_mode)
    cosine, sine = (both[:count], both[count:])
    return join_parts(cosine[..., 0] + sine[..., 1], cosine[..., 1] - sine[..., 0])


def synth_rows(modes, table):
    count = modes.shape[0]
    shaped = modes.reshape(modes.shape[:-1] + (modes.shape[-1] // 2, 2))
    cosine = jnp.einsum("kh,kbomp->bohmp", table[:count], shaped, precision=precise_mode)
    sine = jnp.einsum("kh,kbomp->bohmp", table[count:], shaped, precision=precise_mode)
    return join_parts(cosine[..., 0] - sine[..., 1], cosine[..., 1] + sine[..., 0])


def mix_modes(spectrum, weight):
    spec_re, spec_im = split_parts(spectrum)
    wgt_re, wgt_im = split_parts(weight)

    def contract(left, right):
        return jnp.einsum("kbcm,kcom->kbom", left, right, precision=precise_mode)

    real = contract(spec_re, wgt_re) - contract(spec_im, wgt_im)
    imag = contract(spec_re, wgt_im) + contract(spec_im, wgt_re)
    return join_parts(real, imag)


def mix_grads(spectrum, weight, grad_mixed):
    spec_re, spec_im = split_parts(spectrum)
    wgt_re, wgt_im = split_parts(weight)
    grad_re, grad_im = split_parts(grad_mixed)

    def outer(left, right):
        return jnp.einsum("kbom,kbcm->kcom", left, right, precision=precise_mode)

    def inner(left, right):
        return jnp.einsum("kcom,kbom->kbcm", left, right, precision=precise_mode)

    weight_re = outer(grad_re, spec_re) + outer(grad_im, spec_im)
    weight_im = outer(grad_im, spec_re) - outer(grad_re, spec_im)
    input_re = inner(wgt_re, grad_re) + inner(wgt_im, grad_im)
    input_im = inner(wgt_re, grad_im) - inner(wgt_im, grad_re)
    return (join_parts(weight_re, weight_im), join_parts(input_re, input_im))


def gelu_slope(values):
    cumulative = 0.5 * (1.0 + jax.scipy.special.erf(values / math.sqrt(2.0)))
    density = jnp.exp(-0.5 * values * values) / math.sqrt(2.0 * math.pi)
    return cumulative + values * density


def body(field, cotangent, weight, bias, mode_rows, mode_cols):
    rows_here = field.shape[2]
    row_count = lax.axis_size("rows")
    grid_rows = rows_here * row_count
    grid_cols = field.shape[3]
    all_rows = jnp.arange(grid_rows, dtype=jnp.int32)
    table_w = column_table(mode_cols, grid_cols)
    scale_fwd = 1.0 / math.sqrt(grid_rows * grid_cols)
    scale_inv = 1.0 / math.sqrt(mode_rows.shape[0] * mode_cols.shape[0])

    def analyze(values):
        columns = jnp.dot(
            values, table_w.T, precision=precise_mode, preferred_element_type=jnp.float32
        )
        spread = lax.all_to_all(columns, "rows", split_axis=3, concat_axis=2, tiled=True)
        pieces = analyze_rows(spread, row_table(mode_rows, all_rows, grid_rows))
        return lax.all_to_all(pieces, "rows", split_axis=0, concat_axis=3, tiled=True)

    def synthesize(modes):
        spread = lax.all_to_all(modes, "rows", split_axis=3, concat_axis=0, tiled=True)
        pieces = synth_rows(spread, row_table(mode_rows, all_rows, grid_rows))
        gathered = lax.all_to_all(pieces, "rows", split_axis=2, concat_axis=3, tiled=True)
        return jnp.dot(
            gathered, table_w, precision=precise_mode, preferred_element_type=jnp.float32
        )

    spectrum = analyze(field) * scale_fwd
    mixed = lax.psum_scatter(mix_modes(spectrum, weight), "ch", scatter_dimension=2, tiled=True)
    outputs_here = mixed.shape[2]
    bias_here = lax.dynamic_slice_in_dim(bias, lax.axis_index("ch") * outputs_here, outputs_here)
    before = synthesize(mixed) * scale_inv + bias_here[None, :, None, None]
    grad_before = cotangent * gelu_slope(before)
    grad_mixed = analyze(grad_before) * scale_inv
    grad_whole = lax.all_gather(grad_mixed, "ch", axis=2, tiled=True)
    grad_weight, grad_spectrum = mix_grads(spectrum, weight, grad_whole)
    grad_field = synthesize(grad_spectrum) * scale_fwd
    return (grad_field, grad_weight)


def split_bf16(values):
    high = values.astype(jnp.bfloat16)
    low = (values - high.astype(jnp.float32)).astype(jnp.bfloat16)
    return high, low


def turn_cosine(step, length):
    step = lax.rem(step, jnp.int32(length)) if length & (length - 1) else step & (length - 1)
    folded = jnp.abs(step - length // 2) - length // 4
    angle = folded.astype(jnp.float32) * (2.0 * math.pi / length)
    square = angle * angle
    total = jnp.float32(-2.5052108e-08)
    for factor in (2.7557319e-06, -1.9841270e-04, 8.3333333e-03, -1.6666667e-01):
        total = total * square + factor
    return angle + angle * square * total


def next_lane(values):
    return pltpu.roll(values, values.shape[-1] - 1, values.ndim - 1)


def prev_lane(values):
    return pltpu.roll(values, 1, values.ndim - 1)


def even_lanes(values):
    return lax.broadcasted_iota(jnp.int32, values.shape, values.ndim - 1) % 2 == 0


def swap_pairs(values):
    return jnp.where(even_lanes(values), next_lane(values), prev_lane(values))


def swap_rows(values, distance):
    row = lax.broadcasted_iota(jnp.int32, values.shape, 0)
    ahead = pltpu.roll(values, values.shape[0] - distance, 0)
    behind = pltpu.roll(values, distance, 0)
    return jnp.where(row // distance % 2 == 0, ahead, behind)


def row_sums(tiles):
    count = len(tiles)
    row = lax.broadcasted_iota(jnp.int32, tiles[0].shape, 0)
    while len(tiles) > 1:
        half = len(tiles) // 2
        first = row // half % 2 == 0
        merged = []
        for one, two in zip(tiles[:half], tiles[half:]):
            stay, move = jnp.where(first, one, two), jnp.where(first, two, one)
            moved = pltpu.roll(move, half, 0) if 2 * half == count else swap_rows(move, half)
            merged.append(stay + moved)
        tiles = merged
    return tiles[0]


def layer_kernel(
    sizes, field_hbm, cot_hbm, weight_hbm, small_hbm,
    gfield_ref, same_ref, cross_ref, grads_ref,
    gswap_ref, weight_ref, field_ref, cot_ref, small_ref,
    analysis_ref, synthesis_ref, fwd_ref, inv_ref, stack_ref,
    few_ref, many_ref, part_ref, arrive_ref, gall_ref, acc_ref,
    local_sem, field_sem, send_sem, recv_sem, ch_send, ch_recv,
):
    samples, chans, rows_here, width, kept, ranks, groups, lanes = sizes
    grid_rows = rows_here * ranks
    kept_here = kept // ranks
    handlers = ranks // samples
    own_chans = chans // handlers
    flat_rows = chans * rows_here
    scale_fwd = 1.0 / math.sqrt(grid_rows * width)
    scale_inv = 1.0 / math.sqrt(kept * (lanes // 2))
    me, mine = lax.axis_index("rows"), lax.axis_index("ch")
    my_sample, my_slot = lax.rem(me, samples), me // samples
    mesh_ids = pl.DeviceIdType.MESH

    def rank_at(step):
        return lax.rem(me + step, ranks)

    def group_at(step):
        return lax.rem(mine + step, groups)

    barrier = pltpu.get_barrier_semaphore()
    for step in range(1, ranks):
        pl.semaphore_signal(barrier, inc=1, device_id=(rank_at(step), mine), device_id_type=mesh_ids)
    for step in range(1, groups):
        pl.semaphore_signal(barrier, inc=1, device_id=(me, group_at(step)), device_id_type=mesh_ids)

    load_small = pltpu.make_async_copy(small_hbm, small_ref, local_sem.at[0])
    load_small.start()

    def row_copies(source, target, kind):
        found = []
        for b in range(samples):
            for h in range(rows_here):
                copy = pltpu.make_async_copy(
                    source.at[b, :, h, :], target.at[b, h], field_sem.at[kind, b, h]
                )
                copy.start()
                found.append(copy)
        return found

    load_field = row_copies(field_hbm, field_ref, 0)
    load_weight = pltpu.make_async_copy(weight_hbm, weight_ref, local_sem.at[1])
    load_weight.start()
    load_cot = row_copies(cot_hbm, cot_ref, 1)
    load_small.wait()

    def as_column(values):
        count = values.shape[1]
        row = lax.broadcasted_iota(jnp.int32, (count, count), 0)
        lane = lax.broadcasted_iota(jnp.int32, (count, count), 1)
        kept_values = jnp.where(row == lane, values.astype(jnp.float32), 0.0)
        return jnp.sum(kept_values, axis=1, keepdims=True)

    def pick(column, index):
        row = lax.broadcasted_iota(jnp.int32, (column.shape[0], index.shape[1]), 0)
        return jnp.sum(jnp.where(row == index, column, 0.0), axis=0, keepdims=True).astype(jnp.int32)

    col_column = as_column(small_ref[1:2, :lanes // 2])
    col_lanes = pick(col_column, lax.broadcasted_iota(jnp.int32, (1, lanes), 1) // 2)
    row_column = as_column(small_ref[2:3, :kept])
    row_lanes = pick(row_column, lax.broadcasted_iota(jnp.int32, (1, 6 * kept), 1) % kept)
    row_column = row_column.astype(jnp.int32)
    chunk = 128

    @pl.loop(0, width // chunk)
    def _(at):
        shape = (chunk, lanes)
        column = lax.broadcasted_iota(jnp.int32, shape, 0) + at * chunk
        quarter = lax.broadcasted_iota(jnp.int32, shape, 1) % 2 * (width // 4)
        high, low = split_bf16(turn_cosine(col_lanes * column + quarter, width))
        here = pl.ds(pl.multiple_of(at * chunk, chunk), chunk)
        analysis_ref[here, :lanes] = high
        analysis_ref[here, lanes:] = low

    def fill_synthesis():
        modes = as_column(col_lanes).astype(jnp.int32)

        @pl.loop(0, width // chunk)
        def _(at):
            shape = (lanes, chunk)
            column = lax.broadcasted_iota(jnp.int32, shape, 1) + at * chunk
            quarter = lax.broadcasted_iota(jnp.int32, shape, 0) % 2 * (width // 4)
            high, low = split_bf16(turn_cosine(modes * column + quarter, width))
            here = pl.ds(pl.multiple_of(at * chunk, chunk), chunk)
            synthesis_ref[:lanes, here] = high
            synthesis_ref[lanes:2 * lanes, here] = low
            synthesis_ref[2 * lanes:, here] = high

    def packed_table(step, length):
        table = turn_cosine(step, length)
        high, low = split_bf16(table)
        lane = lax.broadcasted_iota(jnp.int32, table.shape, 1)
        edge = table.shape[1] // 3 * 2
        chosen = jnp.where(lane < edge, high.astype(jnp.float32), low.astype(jnp.float32))
        return chosen.astype(jnp.bfloat16)

    spot = lax.broadcasted_iota(jnp.int32, (kept, 6 * grid_rows), 1)
    turn = spot // grid_rows % 2 * (3 * grid_rows // 4)
    fwd_ref[...] = packed_table(row_column * (spot % grid_rows) + turn, grid_rows)
    spot = lax.broadcasted_iota(jnp.int32, (grid_rows, 6 * kept), 1)
    turn = spot // kept % 2 * (grid_rows // 4)
    row = lax.broadcasted_iota(jnp.int32, (grid_rows, 6 * kept), 0)
    inv_ref[...] = packed_table(row_lanes * row + turn, grid_rows)
    whole = small_ref.shape[1]
    out_chan = mine * chans + lax.broadcasted_iota(jnp.int32, (flat_rows, whole), 0) % chans
    picked = lax.broadcasted_iota(jnp.int32, (flat_rows, whole), 1) == out_chan
    bias_rows = jnp.sum(jnp.where(picked, small_ref[0:1, :], 0.0), axis=1, keepdims=True)

    def analyze_cols(values):
        high, low = split_bf16(values.reshape(flat_rows, width))
        both = jnp.concatenate([high, low], axis=0)
        result = jnp.dot(both, analysis_ref[...], preferred_element_type=jnp.float32)
        top = result[:flat_rows, :lanes] + (
            result[:flat_rows, lanes:] + result[flat_rows:, :lanes]
        )
        return top.reshape(rows_here, chans, lanes)

    def synth_cols(values):
        high, low = split_bf16(values.reshape(flat_rows, lanes))
        packed = jnp.concatenate([high, high, low], axis=1)
        return jnp.dot(packed, synthesis_ref[...], preferred_element_type=jnp.float32)

    def block(rank, size):
        return pl.ds(pl.multiple_of(rank * size, size), size)

    def row_copy(phase, source, target, peer, origin):
        return pltpu.make_async_remote_copy(
            src_ref=source, dst_ref=target,
            send_sem=send_sem.at[phase, peer], recv_sem=recv_sem.at[phase, origin],
            device_id=(peer, mine), device_id_type=mesh_ids,
        )

    at_end = []

    def spread(phase, b):
        few, many = few_ref.at[phase, b], many_ref.at[phase]
        size = few.shape[0]

        def copy_to(slot):
            return row_copy(
                phase, few.at[:, block(slot, own_chans), :], many.at[block(me, size)],
                slot * samples + b, me,
            )

        def each(act):
            for step in range(1, handlers):
                act(copy_to(lax.rem(my_slot + step, handlers)))

            @pl.when(my_sample != b)
            def _():
                act(copy_to(my_slot))

        each(lambda copy: copy.start())
        at_end.append(lambda: each(lambda copy: copy.wait_send()))

        @pl.when(my_sample == b)
        def _():
            many[block(me, size)] = few[:, block(my_slot, own_chans), :]

    def transform(phase, b, table_ref, scale):
        @pl.when(my_sample == b)
        def _():
            source, result_ref = many_ref.at[phase], many_ref.at[phase + 1]
            count = source.shape[0]
            size = count // ranks
            for step in range(1, ranks):
                origin = rank_at(step)
                here = source.at[block(origin, size)]
                row_copy(phase, here, here, origin, origin).wait_recv()
            for pair in range(own_chans):
                values = source[:, pair, :]
                crossed = jnp.where(even_lanes(values), next_lane(values), -prev_lane(values))
                here = slice(pair * lanes, (pair + 1) * lanes)
                for at, piece in enumerate((values, crossed)):
                    high, low = split_bf16(piece)
                    stack_ref[at * count:(at + 1) * count, here] = high
                    stack_ref[(2 + at) * count:(3 + at) * count, here] = low
                    stack_ref[(4 + at) * count:(5 + at) * count, here] = high
            result = jnp.dot(table_ref[...], stack_ref[...], preferred_element_type=jnp.float32)
            result = result * scale
            for pair in range(own_chans):
                result_ref[:, pair, :] = result[:, pair * lanes:(pair + 1) * lanes]
            few = few_ref.at[phase + 1, b]
            for step in range(1, ranks):
                peer = rank_at(step)
                row_copy(
                    phase + 1, result_ref.at[block(peer, size)],
                    few.at[:, block(my_slot, own_chans), :], peer, me,
                ).start()
            few[:, block(my_slot, own_chans), :] = result_ref[block(me, size)]

        def finish():
            @pl.when(my_sample == b)
            def _():
                size = many_ref.shape[1] // ranks
                for step in range(1, ranks):
                    peer = rank_at(step)
                    here = many_ref.at[phase + 1, block(peer, size)]
                    row_copy(phase + 1, here, here, peer, me).wait_send()

        at_end.append(finish)

    def collected(phase, b):
        few = few_ref.at[phase, b]

        def arrived(slot):
            here = few.at[:, block(slot, own_chans), :]
            origin = slot * samples + b
            row_copy(phase, here, here, origin, origin).wait_recv()

        for step in range(1, handlers):
            arrived(lax.rem(my_slot + step, handlers))

        @pl.when(my_sample != b)
        def _():
            arrived(my_slot)

        return few

    def mix_group(b, group, out_ref):
        outs = pl.ds(pl.multiple_of(group * chans, chans), chans)

        @pl.loop(0, kept_here)
        def _(k):
            plain = jnp.zeros((chans, lanes), jnp.float32)
            turned = jnp.zeros((chans, lanes), jnp.float32)
            for c in range(chans):
                w = weight_ref[k, c, outs, :]
                at = b * chans + c
                plain = plain + w * same_ref[k, at:at + 1, :]
                turned = turned + w * cross_ref[k, at:at + 1, :]
            out_ref[k] = plain + swap_pairs(turned)

    def group_copy(kind, b, step, source, target):
        return pltpu.make_async_remote_copy(
            src_ref=source, dst_ref=target,
            send_sem=ch_send.at[kind, b, step - 1], recv_sem=ch_recv.at[kind, b, step - 1],
            device_id=(me, group_at(step)), device_id_type=mesh_ids,
        )

    order = sorted(range(1, groups), key=lambda step: -min(step, groups - step))
    tile = 8

    def back_group(b, group, grad_ref, fresh, last):
        here = slice(b * chans, (b + 1) * chans)
        for k in range(kept_here):
            values = grad_ref[k]
            grads_ref[group, k, here, :] = values
            gswap_ref[group, k, here, :] = swap_pairs(values)

        @pl.loop(0, kept_here * (chans // tile))
        def _(at):
            k, first = at // (chans // tile), at % (chans // tile) * tile
            sums = [[None, None] for _ in range(tile)]
            for o in range(0, chans, tile):
                row = slice(b * chans + o, b * chans + o + tile)
                factors = (grads_ref[group, k, row, :], gswap_ref[group, k, row, :])
                outs = pl.ds(pl.multiple_of(group * chans + o, tile), tile)
                for c in range(tile):
                    w = weight_ref[k, first + c, outs, :]
                    for i, factor in enumerate(factors):
                        term = w * factor
                        sums[c][i] = term if sums[c][i] is None else sums[c][i] + term
            for i in range(2):
                for c in range(tile):
                    if not fresh:
                        sums[c][i] = sums[c][i] + acc_ref[b, at, i, c]
                    if not last:
                        acc_ref[b, at, i, c] = sums[c][i]
            if last:
                p, q = (row_sums([pair[i] for pair in sums]) for i in range(2))
                into = pl.ds(pl.multiple_of(first, tile), tile)
                few_ref[6, b, k, into, :] = jnp.where(
                    even_lanes(p), p + next_lane(p), prev_lane(q) - q
                )

    def flow(b):
        for copy in load_field[b * rows_here:(b + 1) * rows_here]:
            copy.wait()
        few_ref[0, b] = analyze_cols(field_ref[b])
        if b == 0:
            pl.semaphore_wait(barrier, ranks - 1 + groups - 1)
        spread(0, b)
        if b == samples - 1:
            fill_synthesis()
        yield
        transform(0, b, fwd_ref, scale_fwd)
        yield
        spectrum = collected(1, b)
        here = slice(b * chans, (b + 1) * chans)
        for k in range(kept_here):
            values = spectrum[k]
            even = even_lanes(values)
            same_ref[k, here, :] = jnp.where(even, values, prev_lane(values))
            cross_ref[k, here, :] = jnp.where(even, next_lane(values), -values)
        if b == 0:
            load_weight.wait()
        copies = []
        for step in order:
            part = part_ref.at[b, step - 1]
            mix_group(b, group_at(step), part)
            copy = group_copy(0, b, step, part, arrive_ref.at[b, step - 1])
            copy.start()
            copies.append(copy)
        mixed = few_ref.at[2, b]
        mix_group(b, mine, mixed)
        at_end.extend(copy.wait_send for copy in copies)
        yield
        for copy in copies:
            copy.wait_recv()
        for k in range(kept_here):
            total = mixed[k]
            for step in order:
                total = total + arrive_ref[b, step - 1, k]
            mixed[k] = total
        spread(2, b)
        yield
        transform(2, b, inv_ref, scale_inv)
        yield
        few = collected(3, b)
        for copy in load_cot[b * rows_here:(b + 1) * rows_here]:
            copy.wait()
        before = synth_cols(few[...]) + bias_rows
        slope = 0.5 * (1.0 + lax.erf(before * (1.0 / math.sqrt(2.0))))
        slope = slope + before * jnp.exp(-0.5 * before * before) * (1.0 / math.sqrt(2.0 * math.pi))
        few_ref[4, b] = analyze_cols(cot_ref[b].reshape(flat_rows, width) * slope)
        spread(4, b)
        yield
        transform(4, b, fwd_ref, scale_inv)
        yield
        own = collected(5, b)
        copies = []
        for step in order:
            copy = group_copy(1, b, step, own, gall_ref.at[b, mine])
            copy.start()
            copies.append(copy)
        at_end.extend(copy.wait_send for copy in copies)
        back_group(b, mine, own, True, groups == 1)
        yield
        near = sorted(order, key=lambda step: min(step, groups - step))
        for step in near:
            copies[order.index(step)].wait_recv()
            source = lax.rem(mine + groups - step, groups)
            back_group(b, source, gall_ref.at[b, source], False, step == near[-1])
        spread(6, b)
        yield
        transform(6, b, inv_ref, scale_fwd)
        yield
        few = collected(7, b)
        gfield_ref[b] = synth_cols(few[...]).reshape(rows_here, chans, width)

    flows = [flow(b) for b in range(samples)]
    for _ in range(11):
        for one in flows:
            next(one, None)
    for act in at_end:
        act()


def output_kernel(
    same_ref, cross_ref, grads_ref, rows_hbm, gfield_hbm, gweight_hbm,
    gweight_ref, gswap_ref, field_sem, weight_sem,
):
    samples, rows_here, chans = rows_hbm.shape[:3]
    groups, kept_here = grads_ref.shape[:2]
    tile, together, count = 8, 2, 8
    copies = []
    for b in range(samples):
        for h in range(rows_here):
            copy = pltpu.make_async_copy(
                rows_hbm.at[b, h], gfield_hbm.at[b, :, h, :], field_sem.at[b, h]
            )
            copy.start()
            copies.append(copy)

    @pl.loop(0, kept_here)
    def _(k):
        for group in range(groups):
            gswap_ref[group, k] = swap_pairs(grads_ref[group, k])

    def weight_copy(at):
        k, first = at // (chans // count), at % (chans // count) * count
        here = pl.ds(first, count)
        return pltpu.make_async_copy(
            gweight_ref.at[k, here], gweight_hbm.at[k, here], weight_sem.at[at]
        )

    @pl.loop(0, kept_here * (chans // count))
    def _(at):
        k, first = at // (chans // count), at % (chans // count) * count
        for c in range(0, count, together):
            same, cross = [
                [
                    [ref[k, pl.ds(b * chans + first + c + i, 1), :] for b in range(samples)]
                    for i in range(together)
                ]
                for ref in (same_ref, cross_ref)
            ]
            for group in range(groups):
                for o in range(0, chans, tile):
                    rows = [slice(b * chans + o, b * chans + o + tile) for b in range(samples)]
                    plain = [grads_ref[group, k, row, :] for row in rows]
                    turned = [gswap_ref[group, k, row, :] for row in rows]
                    out = group * chans + o
                    for i in range(together):
                        total = plain[0] * same[i][0] + turned[0] * cross[i][0]
                        for b in range(1, samples):
                            total = total + plain[b] * same[i][b] + turned[b] * cross[i][b]
                        gweight_ref[k, first + c + i, out:out + tile, :] = total
        weight_copy(at).start()

    @pl.loop(0, kept_here * (chans // count))
    def _(at):
        weight_copy(at).wait()

    for copy in copies:
        copy.wait()


def kernel_fits(ranks, groups, field, weight, mode_rows, bias):
    pairs = field.shape[0] * field.shape[1]
    lanes = weight.shape[3]
    return (
        pairs % (8 * ranks) == 0 and ranks % field.shape[0] == 0 and lanes == 128 and field.shape[1] % 8 == 0
        and field.shape[1] * groups == weight.shape[2] and mode_rows.shape[0] % 32 == 0
        and field.shape[2] * ranks % 32 == 0 and mode_rows.shape[0] == field.shape[2] * ranks
        and field.shape[3] % 128 == 0 and bias.shape[0] % 128 == 0
    )


def kernel_body(field, cotangent, weight, bias, mode_rows, mode_cols):
    samples, chans, rows_here, width = field.shape
    ranks, groups = lax.axis_size("rows"), lax.axis_size("ch")
    kept, lanes = mode_rows.shape[0], weight.shape[3]
    grid_rows = rows_here * ranks
    kept_here = kept // ranks
    pairs = samples * chans
    own_chans = pairs // ranks
    f32, bf16 = jnp.float32, jnp.bfloat16
    small = jnp.stack([
        jnp.pad(values.astype(f32), (0, bias.shape[0] - values.shape[0]))
        for values in (bias, mode_cols, mode_rows)
    ])
    sizes = (samples, chans, rows_here, width, kept, ranks, groups, lanes)
    vmem = pl.BlockSpec(memory_space=pltpu.VMEM)
    hbm = pl.BlockSpec(memory_space=pltpu.HBM)
    modes = (kept_here, pairs, lanes)
    slab = (kept_here, chans, lanes)
    by_row = (samples, rows_here, chans, width)
    dma = pltpu.SemaphoreType.DMA
    rows, same, cross, grads = pl.pallas_call(
        functools.partial(layer_kernel, sizes),
        out_shape=(
            jax.ShapeDtypeStruct(by_row, f32),
            jax.ShapeDtypeStruct(modes, f32),
            jax.ShapeDtypeStruct(modes, f32),
            jax.ShapeDtypeStruct((groups,) + modes, f32),
        ),
        in_specs=[hbm] * 4,
        out_specs=(vmem,) * 4,
        scratch_shapes=[
            pltpu.VMEM((groups,) + modes, f32),
            pltpu.VMEM(weight.shape, f32),
            pltpu.VMEM(by_row, f32),
            pltpu.VMEM(by_row, f32),
            pltpu.VMEM(small.shape, f32),
            pltpu.VMEM((width, 2 * lanes), bf16),
            pltpu.VMEM((3 * lanes, width), bf16),
            pltpu.VMEM((kept, 6 * grid_rows), bf16),
            pltpu.VMEM((grid_rows, 6 * kept), bf16),
            pltpu.VMEM((6 * kept, own_chans * lanes), bf16),
            pltpu.VMEM((8, samples) + slab, f32),
            pltpu.VMEM((8, grid_rows, own_chans, lanes), f32),
            pltpu.VMEM((samples, groups - 1) + slab, f32),
            pltpu.VMEM((samples, groups - 1) + slab, f32),
            pltpu.VMEM((samples, groups) + slab, f32),
            pltpu.VMEM((samples, kept_here * chans // 8, 2, 8, 8, lanes), f32),
            dma((2,)),
            dma((2, samples, rows_here)),
            dma((8, ranks)),
            dma((8, ranks)),
            dma((2, samples, groups - 1)),
            dma((2, samples, groups - 1)),
        ],
        compiler_params=pltpu.CompilerParams(
            collective_id=0, has_side_effects=True, vmem_limit_bytes=52 * 1024 * 1024
        ),
    )(
        field, cotangent, weight, small,
    )
    gfield, gweight = pl.pallas_call(
        output_kernel,
        out_shape=(
            jax.ShapeDtypeStruct(field.shape, f32), jax.ShapeDtypeStruct(weight.shape, f32),
        ),
        in_specs=[vmem] * 3 + [pl.BlockSpec(memory_space=pl.ANY)],
        out_specs=(hbm, hbm),
        scratch_shapes=[
            pltpu.VMEM(weight.shape, f32),
            pltpu.VMEM(grads.shape, f32),
            dma((samples, rows_here)),
            dma((kept_here * chans // 8,)),
        ],
        compiler_params=pltpu.CompilerParams(vmem_limit_bytes=32 * 1024 * 1024),
    )(same, cross, grads, rows)
    return gfield, gweight


def any_body(field, cotangent, weight, bias, mode_rows, mode_cols):
    ranks, groups = lax.axis_size("rows"), lax.axis_size("ch")
    chosen = kernel_body if kernel_fits(ranks, groups, field, weight, mode_rows, bias) else body
    return chosen(field, cotangent, weight, bias, mode_rows, mode_cols)


def solution(mesh):
    return jax.shard_map(
        any_body,
        mesh=mesh,
        in_specs=(
            P(None, "ch", "rows", None),
            P(None, "ch", "rows", None),
            P("rows", "ch", None, None),
            P(),
            P(),
            P(),
        ),
        out_specs=(P(None, "ch", "rows", None), P("rows", "ch", None, None)),
        check_vma=False,
    )
```
